32 devices in a mesh: group: 2 (over y), tm: 8 (over z, core), pix: 2 (over x), sub: 1.
Axes of the slice: x: 2, y: 2, z: 4, core: 2. Of those that a mesh axis runs over, the one named last changes fastest.
Arguments:
- anomaly: bfloat16 [512, 65536], P('tm', ('group', 'pix', 'sub')), parts along dimension 1, may hold values from -6 to 6
- offsets: int32 [32], replicated, may hold values from 0 to 256, as said below
- taper_index: int32 [32], replicated, may hold values from 0 to 3
Outputs:
- spectral_gram: float32 [256, 64, 64], P(('group', 'tm')), parts along dimension 0
- leading_energy: float32 [256], P(('group', 'tm')), parts along dimension 0
The draws below stay inside these ranges and needn't reach their ends.
There are 2 independent parts, one for each index of `group`. The reference program is written for one: setup_inputs(seed, part) draws one part's arguments, and reference() takes and returns one part's arrays. A program takes and returns all parts, laid end to end along the dimension named above; an argument that names none is the same for every part. Nothing has to cross between parts.
Inputs may be any that keep to these rules, and one draw needn't show every extreme that they name: `offsets`: block starts never fall; the first block starts at day 0 and the last at day 512 - 256.
All inputs are finite; a program needn't handle non-finite values.
Results may differ from the reference program's by a relative error of at most 0.0034.
Values may be sent and summed in bfloat16 or wider, within the bound.
No kernel may reach another device: no remote copies, remote signals or barrier semaphores. Data moves between devices by JAX's collectives and lax.ppermute only.
A program may use at most 128 MiB of HBM per device.

```python
import math
import jax
import jax.numpy as jnp
from jax import lax

NFFT = 256
NB = 32
POWER = 8
PIX_DEV = 16384
NF = 128
DAYS = 512
PIXELS = 32768


def draw_offsets(key, part):
    stride = (DAYS - NFFT) // (NB - 1)
    jitter = jax.random.randint(key, (NB,), 0, stride // 2 + 1)
    blocks = jnp.arange(NB, dtype=jnp.int32)
    starts = blocks * stride + jitter.astype(jnp.int32)
    starts = jnp.where(blocks == 0, 0, starts)
    starts = jnp.where(blocks == NB - 1, DAYS - NFFT, starts)
    return starts.astype(jnp.int32)


def set_ends(values, rng, smallest, top_value):
    dims = values.shape
    place = [jax.random.randint(jax.random.fold_in(rng, axis), (), 0, dims[axis]) for axis in range(len(dims))]
    values = values.at[tuple(place)].set(smallest)
    longest = dims.index(max(dims))
    place[longest] = (place[longest] + 1) % dims[longest]
    return values.at[tuple(place)].set(top_value)


def levels(key, extent, pieces, smallest, largest):
    def one(position, blocks):
        steps = jax.random.uniform(jax.random.fold_in(jax.random.fold_in(key, 6), position), (blocks,), jnp.float32, smallest / len(pieces), largest / len(pieces))
        return jnp.repeat(jnp.exp(steps), extent[position] // blocks).reshape((-1,) + (1,) * (len(extent) - position - 1))

    loudness = one(*pieces[0])
    for cut in pieces[1:]:
        loudness = loudness * one(*cut)
    return loudness


def scatter_about(rng, shape, scale, bound, pieces=(), kind=jnp.bfloat16):
    result = scale * jax.random.normal(rng, shape, jnp.float32)
    if pieces:
        result = result * levels(rng, shape, pieces, -0.22, 0.18)
    return jnp.clip(result, -bound, bound).astype(kind)


def setup_inputs(seed: int = 0, part: int = 0) -> dict:
    streams_of = jax.random.split(jax.random.key(seed), 4)
    part_keys = jax.random.split(jax.random.fold_in(streams_of[3], part), 4)
    anomaly = scatter_about(part_keys[0], (DAYS, PIXELS), 1.0, 6.0, ((0, 8), (1, 2)))
    offsets = draw_offsets(jax.random.fold_in(streams_of[3], 71), part)
    taper_index = set_ends(jax.random.randint(streams_of[2], (NB,), 0, 4), jax.random.fold_in(streams_of[2], 1), 0, 3).astype(jnp.int32)
    return dict(anomaly=anomaly, offsets=offsets, taper_index=taper_index)


power_eps = 1e-06

def window_rows(taper_index, length):
    steps_t = jnp.arange(length, dtype=jnp.float32)
    phase = steps_t * (2.0 * math.pi / length)
    center = (steps_t + 0.5) * (math.pi / length)
    hann = jnp.sin(center) ** 2
    hamming = 0.54 - 0.46 * jnp.cos(phase)
    blackman = 0.42 - 0.5 * jnp.cos(phase) + 0.08 * jnp.cos(2.0 * phase)
    sine_win = jnp.sin(center)
    table_rows = jnp.stack([hann, hamming, blackman, sine_win])
    chosen = jnp.zeros((taper_index.shape[0], length), jnp.float32)
    for which in range(4):
        chosen = chosen + jnp.where(taper_index[:, None] == which, table_rows[which][None, :], jnp.float32(0.0))
    return chosen

def dft_table(length, kept):
    freqs = jnp.arange(kept, dtype=jnp.int32)
    times = jnp.arange(length, dtype=jnp.int32)
    product = freqs[:, None] * times[None, :] % length
    angle = product.astype(jnp.float32) * (2.0 * math.pi / length)
    return jnp.stack([jnp.cos(angle), -jnp.sin(angle)]).astype(jnp.bfloat16)

def reference(anomaly, offsets, taper_index):
    windows = window_rows(taper_index, NFFT)
    energy = 1.0 / jnp.sqrt(lax.optimization_barrier(jnp.sum(windows * windows, axis=1)))
    transform = dft_table(NFFT, NF).astype(jnp.float32)
    spans = PIXELS // PIX_DEV

    def one_span(running, span_index):
        columns = lax.dynamic_slice_in_dim(anomaly, (span_index * PIX_DEV).astype(jnp.int32), PIX_DEV, 1)
        segments = jax.vmap(lambda first_day: lax.dynamic_slice_in_dim(columns, first_day.astype(jnp.int32), NFFT, 0))(offsets)
        windowed = (segments.astype(jnp.float32) * windows[:, :, None]).astype(jnp.bfloat16)
        spectra = jnp.einsum('rkt,btp->rbkp', transform, windowed.astype(jnp.float32))
        spectra = (spectra * energy[None, :, None, None]).astype(jnp.bfloat16)
        stacked = spectra.reshape(2 * NB, NF, PIX_DEV).astype(jnp.float32)
        return (running + jnp.einsum('ifp,jfp->fij', stacked, stacked), None)
    start_sum = jnp.zeros((NF, 2 * NB, 2 * NB), jnp.float32)
    summed, _ = lax.scan(one_span, start_sum, jnp.arange(spans, dtype=jnp.int32))
    spectral_gram = summed / PIXELS
    vector = jnp.ones((NF, 2 * NB), jnp.float32)
    for _ in range(POWER):
        applied = jnp.einsum('fij,fj->fi', spectral_gram, vector, precision=lax.Precision.HIGHEST)
        vector = applied / jnp.sqrt(lax.optimization_barrier(jnp.mean(applied * applied, axis=1, keepdims=True)) + power_eps)
    applied = jnp.einsum('fij,fj->fi', spectral_gram, vector, precision=lax.Precision.HIGHEST)
    leading_energy = jnp.sqrt(lax.optimization_barrier(jnp.mean(applied * applied, axis=1)))
    return (spectral_gram, leading_energy)
```

```python
import functools
import math

import jax
import jax.numpy as jnp
import numpy as np
from jax import lax
from jax.experimental import pallas as pl
from jax.experimental.pallas import tpu as pltpu
from jax.sharding import PartitionSpec as P

NFFT = 256
NB = 32
POWER = 8
NF = 128
TILE = 128
VMEM_BYTES = 40 * 1024 * 1024

power_eps = 1e-06


def window_rows(taper_index, length):
    steps_t = jnp.arange(length, dtype=jnp.float32)
    phase = steps_t * (2.0 * math.pi / length)
    center = (steps_t + 0.5) * (math.pi / length)
    hann = jnp.sin(center) ** 2
    hamming = 0.54 - 0.46 * jnp.cos(phase)
    blackman = 0.42 - 0.5 * jnp.cos(phase) + 0.08 * jnp.cos(2.0 * phase)
    sine_win = jnp.sin(center)
    table_rows = jnp.stack([hann, hamming, blackman, sine_win])
    chosen = jnp.zeros((taper_index.shape[0], length), jnp.float32)
    for which in range(4):
        chosen = chosen + jnp.where(
            taper_index[:, None] == which, table_rows[which][None, :], jnp.float32(0.0)
        )
    return chosen


def dft_table(length, kept):
    freqs = jnp.arange(kept, dtype=jnp.int32)
    times = jnp.arange(length, dtype=jnp.int32)
    product = freqs[:, None] * times[None, :] % length
    angle = product.astype(jnp.float32) * (2.0 * math.pi / length)
    return jnp.stack([jnp.cos(angle), -jnp.sin(angle)]).astype(jnp.bfloat16)


def local_gram(spectra):
    stacked = spectra.reshape(2 * spectra.shape[1], spectra.shape[2], spectra.shape[3])
    return jnp.einsum("ifp,jfp->fij", stacked, stacked, preferred_element_type=jnp.float32)


def spectra_shards(anomaly, offsets, taper_index):
    series = lax.all_to_all(anomaly, "tm", split_axis=1, concat_axis=0, tiled=True)
    windows = window_rows(taper_index, NFFT)
    energy = 1.0 / jnp.sqrt(jnp.sum(windows * windows, axis=1))
    transform = dft_table(NFFT, NF)
    width_here = series.shape[1]
    per_group = 8
    gram_width = 2 * NB

    def fill_group(position, buffer):
        first_block = position * per_group
        starts = lax.dynamic_slice_in_dim(offsets, first_block, per_group, 0)
        shapes = lax.dynamic_slice_in_dim(windows, first_block, per_group, 0)
        scales = lax.dynamic_slice_in_dim(energy, first_block, per_group, 0)
        segments = jax.vmap(lambda first_day: lax.dynamic_slice_in_dim(series, first_day, NFFT, 0))(
            starts
        )
        windowed = (segments * shapes[:, :, None]).astype(jnp.bfloat16)
        spectra = jnp.einsum(
            "rkt,btp->rbkp", transform, windowed, preferred_element_type=jnp.float32
        )
        spectra = (spectra * scales[None, :, None, None]).astype(jnp.bfloat16)
        return lax.dynamic_update_slice_in_dim(buffer, spectra, first_block, 1)

    empty = jnp.zeros((2, NB, NF, width_here), jnp.bfloat16)
    spectra = lax.fori_loop(0, NB // per_group, fill_group, empty)
    received = lax.all_to_all(spectra, "tm", split_axis=2, concat_axis=3, tiled=True)
    partial_value = local_gram(received)
    summed = lax.psum(partial_value, ("pix", "sub"))
    total_pixels = anomaly.shape[1] * lax.axis_size(("pix", "sub"))
    spectral_gram = summed / total_pixels
    vector = jnp.ones((spectral_gram.shape[0], gram_width), jnp.float32)
    for _ in range(POWER):
        applied = jnp.einsum("fij,fj->fi", spectral_gram, vector, precision=lax.Precision.HIGHEST)
        vector = applied / jnp.sqrt(jnp.mean(applied * applied, axis=1, keepdims=True) + power_eps)
    applied = jnp.einsum("fij,fj->fi", spectral_gram, vector, precision=lax.Precision.HIGHEST)
    leading_energy = jnp.sqrt(jnp.mean(applied * applied, axis=1))
    return (spectral_gram, leading_energy)


def day_factors(days):
    return (1.0 + 0.4 * ((np.arange(days) * 0.6180339887498949) % 1.0)).astype(np.float32)


def upper_tiles(days):
    count = days // TILE
    return [(i, j) for i in range(count) for j in range(i, count)]


def weights(offsets, taper_index, first_freq, freqs, days):
    local = jnp.arange(days, dtype=jnp.int32)[None, :] - offsets[:, None]
    inside = (local >= 0) & (local < NFFT)
    steps_t = local.astype(jnp.float32)
    phase = steps_t * (2.0 * math.pi / NFFT)
    center = (steps_t + 0.5) * (math.pi / NFFT)
    sine_win = jnp.sin(center)
    table = [
        sine_win**2,
        0.54 - 0.46 * jnp.cos(phase),
        0.42 - 0.5 * jnp.cos(phase) + 0.08 * jnp.cos(2.0 * phase),
        sine_win,
    ]
    window = jnp.zeros(local.shape, jnp.float32)
    for which in range(4):
        window = window + jnp.where(taper_index[:, None] == which, table[which], 0.0)
    window = jnp.where(inside, window, 0.0)
    energy = 1.0 / jnp.sqrt(jnp.sum(window * window, axis=1, keepdims=True))
    window = window * energy * (1.0 / day_factors(days))[None, :]

    def turn(steps):
        freq = first_freq + jnp.arange(freqs, dtype=jnp.int32)
        angle = ((freq[:, None] * steps[None, :]) % NFFT).astype(jnp.float32)
        angle = angle * (2.0 * math.pi / NFFT)
        return jnp.cos(angle), jnp.sin(angle)

    cos_t, sin_t = lax.optimization_barrier(turn(jnp.arange(days, dtype=jnp.int32)))
    cos_b, sin_b = lax.optimization_barrier(turn(offsets))
    window = lax.optimization_barrier(window)
    ct, st = cos_t[:, None, :], sin_t[:, None, :]
    cb, sb = cos_b[:, :, None], sin_b[:, :, None]
    real = window * (ct * cb + st * sb)
    imag = window * (ct * sb - st * cb)
    return jnp.concatenate([real, imag], axis=1).astype(jnp.bfloat16)


def covariance_kernel(tiles, place, *refs):
    n = len(refs) - 6
    pieces, (drow, dcol, keep, send, xs, cs) = refs[:n], refs[n:]
    me = place[0]
    rows = pieces[0].shape[0]
    for d in range(n):
        xs[pl.ds(pl.multiple_of((me ^ d) * rows, rows), rows), :] = pieces[d][...]
    for i in range(xs.shape[0] // TILE):
        here = slice(i * TILE, (i + 1) * TILE)
        strip = lax.dot_general(
            xs[here, :], xs[i * TILE :, :], (((1,), (1,)), ((), ())), preferred_element_type=jnp.float32
        )
        strip = strip * dcol[here, :] * drow[:, i * TILE :]
        for u, (a, b) in enumerate(tiles):
            if a == i:
                cs[u] = strip[:, (b - i) * TILE : (b - i + 1) * TILE]
    half = TILE // 2
    core = me % 2
    keep[...] = cs[:, pl.ds(pl.multiple_of(core * half, half), half), :]
    send[...] = cs[:, pl.ds(pl.multiple_of((1 - core) * half, half), half), :].astype(jnp.bfloat16)


def finish_kernel(tiles, scale, place, w, q0, q1, q2, q3, gram, energy, packed, full, y):
    core, pix = place[0] % 2, place[1]
    quarter = TILE // 4
    for source, (c, x) in zip((q0, q1, q2, q3), ((0, 0), (0, 1), (1, 0), (1, 1))):
        at = (core ^ c) * (2 * quarter) + (pix ^ x) * quarter
        packed[:, pl.ds(pl.multiple_of(at, quarter), quarter), :] = source[...]
    for u, (a, b) in enumerate(tiles):
        block = packed[u]
        full[a * TILE : (a + 1) * TILE, b * TILE : (b + 1) * TILE] = block
        if a != b:
            full[b * TILE : (b + 1) * TILE, a * TILE : (a + 1) * TILE] = block.T
    freqs, width, days = w.shape
    flat = w[...].reshape(freqs * width, days)
    y[...] = jnp.dot(flat, full[...], preferred_element_type=jnp.float32).astype(jnp.bfloat16)
    for f in range(freqs):
        gram[f] = scale * lax.dot_general(
            y[f * width : (f + 1) * width, :], w[f], (((1,), (1,)), ((), ())), preferred_element_type=jnp.float32
        )
    g = gram[...]
    vector = jnp.ones((freqs, 1, width), jnp.float32)
    along = 2
    for step in range(POWER + 1):
        applied = jnp.sum(g * vector, axis=along, keepdims=True)
        along = 3 - along
        mean = jnp.sum(applied * applied, axis=along, keepdims=True) * (1.0 / width)
        if step < POWER:
            vector = applied / jnp.sqrt(mean + power_eps)
    energy[...] = jnp.sqrt(mean[:, :, 0])


def covariance_shards(anomaly, offsets, taper_index):
    n = lax.axis_size("tm")
    me, pix = lax.axis_index("tm"), lax.axis_index("pix")
    rows, width = anomaly.shape[0], anomaly.shape[1] // n
    days = rows * n
    freqs = NF // n
    tiles = upper_tiles(days)
    place = jnp.stack([me, pix]).astype(jnp.int32)

    def tm_swap(value, bit):
        return lax.ppermute(value, "tm", [(i, i ^ bit) for i in range(n)])

    def pix_swap(value):
        return lax.ppermute(value, "pix", [(0, 1), (1, 0)])

    pieces = {}
    for d in list(range(n // 2, n)) + list(range(1, n // 2)):
        pieces[d] = tm_swap(lax.dynamic_slice_in_dim(anomaly, (me ^ d) * width, width, 1), d)
    pieces[0] = lax.dynamic_slice_in_dim(anomaly, me * width, width, 1)
    w = weights(offsets, taper_index, me * freqs, freqs, days)

    factors = day_factors(days)
    vmem = pl.BlockSpec(memory_space=pltpu.VMEM)
    smem = pl.BlockSpec(memory_space=pltpu.SMEM)
    params = pltpu.CompilerParams(vmem_limit_bytes=VMEM_BYTES)
    half = (len(tiles), TILE // 2, TILE)
    keep, send = pl.pallas_call(
        functools.partial(covariance_kernel, tiles),
        out_shape=(jax.ShapeDtypeStruct(half, jnp.float32), jax.ShapeDtypeStruct(half, jnp.bfloat16)),
        in_specs=[smem] + [vmem] * (n + 2),
        out_specs=(vmem, vmem),
        scratch_shapes=[
            pltpu.VMEM((days, width), jnp.bfloat16),
            pltpu.VMEM((len(tiles), TILE, TILE), jnp.float32),
        ],
        compiler_params=params,
    )(place, *[pieces[d] for d in range(n)], jnp.asarray(factors[None, :]), jnp.asarray(factors[:, None]))

    summed = keep + tm_swap(send, 1).astype(jnp.float32)
    quarter = TILE // 4
    mine = lax.dynamic_slice_in_dim(summed, pix * quarter, quarter, 1)
    other = lax.dynamic_slice_in_dim(summed, (1 - pix) * quarter, quarter, 1)
    mine = mine + pix_swap(other.astype(jnp.bfloat16)).astype(jnp.float32)
    bit = 2
    while bit < n:
        mine = mine + tm_swap(mine.astype(jnp.bfloat16), bit).astype(jnp.float32)
        bit *= 2
    q0 = mine.astype(jnp.bfloat16)
    q1 = pix_swap(q0)
    q2 = tm_swap(q0, 1)
    q3 = tm_swap(q1, 1)

    gram_width = 2 * NB
    total_pixels = anomaly.shape[1] * lax.axis_size("pix")
    gram, energy = pl.pallas_call(
        functools.partial(finish_kernel, tiles, 1.0 / total_pixels),
        out_shape=(
            jax.ShapeDtypeStruct((freqs, gram_width, gram_width), jnp.float32),
            jax.ShapeDtypeStruct((freqs, 1), jnp.float32),
        ),
        in_specs=[smem] + [vmem] * 5,
        out_specs=(vmem, vmem),
        scratch_shapes=[
            pltpu.VMEM((len(tiles), TILE, TILE), jnp.bfloat16),
            pltpu.VMEM((days, days), jnp.bfloat16),
            pltpu.VMEM((freqs * gram_width, days), jnp.bfloat16),
        ],
        compiler_params=params,
    )(place, w, q0, q1, q2, q3)
    return gram, energy[:, 0]


def solution(mesh):
    placed = (P("tm", ("group", "pix", "sub")), P(), P())
    n = mesh.shape["tm"]

    def shards(anomaly, offsets, taper_index):
        days = anomaly.shape[0] * n
        pairs = mesh.shape["pix"] == 2 and mesh.shape["sub"] == 1 and n in (2, 4, 8)
        if pairs and days % TILE == 0 and days <= 2 * NFFT:
            return covariance_shards(anomaly, offsets, taper_index)
        return spectra_shards(anomaly, offsets, taper_index)

    return jax.shard_map(
        shards,
        mesh=mesh,
        in_specs=placed,
        out_specs=(P(("group", "tm"), None, None), P(("group", "tm"))),
        check_vma=False,
    )
```

```python
import functools
import math

import jax
import jax.numpy as jnp
import numpy as np
from jax import lax
from jax.experimental import pallas as pl
from jax.experimental.pallas import tpu as pltpu
from jax.sharding import PartitionSpec as P

NFFT = 256
NB = 32
POWER = 8
NF = 128
VMEM_BYTES = 40 * 1024 * 1024
OWN_FLOPS, EARLY_FLOPS, LATE_FLOPS, FINISH_FLOPS = 0, 0, 20_000_000_000, 1_000_000_000

power_eps = 1e-06


def window_rows(taper_index, length):
    steps_t = jnp.arange(length, dtype=jnp.float32)
    phase = steps_t * (2.0 * math.pi / length)
    center = (steps_t + 0.5) * (math.pi / length)
    hann = jnp.sin(center) ** 2
    hamming = 0.54 - 0.46 * jnp.cos(phase)
    blackman = 0.42 - 0.5 * jnp.cos(phase) + 0.08 * jnp.cos(2.0 * phase)
    sine_win = jnp.sin(center)
    table_rows = jnp.stack([hann, hamming, blackman, sine_win])
    chosen = jnp.zeros((taper_index.shape[0], length), jnp.float32)
    for which in range(4):
        chosen = chosen + jnp.where(
            taper_index[:, None] == which, table_rows[which][None, :], jnp.float32(0.0)
        )
    return chosen


def dft_table(length, kept):
    freqs = jnp.arange(kept, dtype=jnp.int32)
    times = jnp.arange(length, dtype=jnp.int32)
    product = freqs[:, None] * times[None, :] % length
    angle = product.astype(jnp.float32) * (2.0 * math.pi / length)
    return jnp.stack([jnp.cos(angle), -jnp.sin(angle)]).astype(jnp.bfloat16)


def local_gram(spectra):
    stacked = spectra.reshape(2 * spectra.shape[1], spectra.shape[2], spectra.shape[3])
    return jnp.einsum("ifp,jfp->fij", stacked, stacked, preferred_element_type=jnp.float32)


def spectra_shards(anomaly, offsets, taper_index):
    series = lax.all_to_all(anomaly, "tm", split_axis=1, concat_axis=0, tiled=True)
    windows = window_rows(taper_index, NFFT)
    energy = 1.0 / jnp.sqrt(jnp.sum(windows * windows, axis=1))
    transform = dft_table(NFFT, NF)
    width_here = series.shape[1]
    per_group = 8
    gram_width = 2 * NB

    def fill_group(position, buffer):
        first_block = position * per_group
        starts = lax.dynamic_slice_in_dim(offsets, first_block, per_group, 0)
        shapes = lax.dynamic_slice_in_dim(windows, first_block, per_group, 0)
        scales = lax.dynamic_slice_in_dim(energy, first_block, per_group, 0)
        segments = jax.vmap(lambda first_day: lax.dynamic_slice_in_dim(series, first_day, NFFT, 0))(
            starts
        )
        windowed = (segments * shapes[:, :, None]).astype(jnp.bfloat16)
        spectra = jnp.einsum(
            "rkt,btp->rbkp", transform, windowed, preferred_element_type=jnp.float32
        )
        spectra = (spectra * scales[None, :, None, None]).astype(jnp.bfloat16)
        return lax.dynamic_update_slice_in_dim(buffer, spectra, first_block, 1)

    empty = jnp.zeros((2, NB, NF, width_here), jnp.bfloat16)
    spectra = lax.fori_loop(0, NB // per_group, fill_group, empty)
    received = lax.all_to_all(spectra, "tm", split_axis=2, concat_axis=3, tiled=True)
    partial_value = local_gram(received)
    summed = lax.psum(partial_value, ("pix", "sub"))
    total_pixels = anomaly.shape[1] * lax.axis_size(("pix", "sub"))
    spectral_gram = summed / total_pixels
    vector = jnp.ones((spectral_gram.shape[0], gram_width), jnp.float32)
    for _ in range(POWER):
        applied = jnp.einsum("fij,fj->fi", spectral_gram, vector, precision=lax.Precision.HIGHEST)
        vector = applied / jnp.sqrt(jnp.mean(applied * applied, axis=1, keepdims=True) + power_eps)
    applied = jnp.einsum("fij,fj->fi", spectral_gram, vector, precision=lax.Precision.HIGHEST)
    leading_energy = jnp.sqrt(jnp.mean(applied * applied, axis=1))
    return (spectral_gram, leading_energy)


def day_factors(days):
    return (1.0 + 0.4 * ((np.arange(days) * 0.6180339887498949) % 1.0)).astype(np.float32)


def day_order(rows):
    blocks = [4 * half + 2 * chip + core for half in (0, 1) for core in (0, 1) for chip in (0, 1)]
    return np.concatenate([np.arange(rows) + rows * block for block in blocks]).astype(np.int32)


def weights(offsets, taper_index, first_freq, freqs, order):
    days = order.shape[0]
    day = jnp.asarray(order)
    local = day[None, :] - offsets[:, None]
    inside = (local >= 0) & (local < NFFT)
    steps_t = local.astype(jnp.float32)
    phase = steps_t * (2.0 * math.pi / NFFT)
    center = (steps_t + 0.5) * (math.pi / NFFT)
    sine_win = jnp.sin(center)
    table = [
        sine_win**2,
        0.54 - 0.46 * jnp.cos(phase),
        0.42 - 0.5 * jnp.cos(phase) + 0.08 * jnp.cos(2.0 * phase),
        sine_win,
    ]
    window = jnp.zeros(local.shape, jnp.float32)
    for which in range(4):
        window = window + jnp.where(taper_index[:, None] == which, table[which], 0.0)
    window = jnp.where(inside, window, 0.0)
    energy = 1.0 / jnp.sqrt(jnp.sum(window * window, axis=1, keepdims=True))
    factors = day_factors(days // 2)
    window = window * energy * (1.0 / np.concatenate([factors, factors]))[None, :]

    def turn(steps):
        freq = first_freq + jnp.arange(freqs, dtype=jnp.int32)
        angle = ((freq[:, None] * steps[None, :]) % NFFT).astype(jnp.float32)
        angle = angle * (2.0 * math.pi / NFFT)
        return jnp.cos(angle), jnp.sin(angle)

    cos_t, sin_t = lax.optimization_barrier(turn(day))
    cos_b, sin_b = lax.optimization_barrier(turn(offsets))
    window = lax.optimization_barrier(window)
    ct, st = cos_t[:, None, :], sin_t[:, None, :]
    cb, sb = cos_b[:, :, None], sin_b[:, :, None]
    real = window * (ct * cb + st * sb)
    imag = window * (ct * sb - st * cb)
    return jnp.concatenate([real, imag], axis=1).astype(jnp.bfloat16)


def outer(left, right):
    return lax.dot_general(left, right, (((1,), (1,)), ((), ())), preferred_element_type=jnp.float32)


def spread(pair, chip):
    low = lax.broadcasted_iota(jnp.int32, pair.shape, 1) < pair.shape[1] // 2
    turned = pltpu.roll(pair, pair.shape[1] // 2, 1)
    first = jnp.where(chip == 0, pair, turned)
    second = jnp.where(chip == 0, turned, pair)
    keep = low == (chip == 0)
    return jnp.concatenate([jnp.where(keep, first, 0.0), jnp.where(keep, second, 0.0)], axis=1)


def block(index, rows):
    return pl.ds(pl.multiple_of(index * rows, rows), rows)


def own_kernel(place, p0, p1, p2a, p2b, p3a, p3b, f0a, f0b, f1a, f1b, drow, dcol, dpair, near, keep, send, pair, strip):
    chip, core = place[1], place[2]
    slot = 2 * core + chip
    rows, middle = p2a.shape
    near[block(slot, rows), :] = p0[...]
    near[block(slot ^ 2, rows), :] = p1[...]
    for flip, first, second in ((1, p2a, p2b), (3, p3a, p3b)):
        near[block(slot ^ flip, rows), :middle] = first[...]
        near[block(slot ^ flip, rows), middle:] = second[...]
    mine = block(core, 2 * rows)
    strip[...] = outer(near[mine, :], near[...]) * (0.5 * dcol[mine, :]) * drow[...]
    width = f0a.shape[1]
    for index, first, second in ((core, f0a, f0b), (1 - core, f1a, f1b)):
        pair[block(index, rows), :width] = first[...]
        pair[block(index, rows), width:] = second[...]
    inside = outer(pair[block(core, rows), :], pair[...]) * (0.5 * dcol[block(slot, rows), :]) * dpair[chip]
    keep[...] = strip[block(chip, rows), :] + spread(inside, chip)
    send[...] = strip[block(1 - chip, rows), :].astype(jnp.bfloat16)


def early_kernel(place, near, early, drow, dcol, out):
    rows = early.shape[0]
    slot = 2 * place[2] + 1 - place[1]
    out[...] = (outer(early[...], near[...]) * dcol[block(slot, rows), :] * drow[...]).astype(jnp.bfloat16)


def late_kernel(place, near, late, e0, e1, before, drow, dcol, dpair, out, pair):
    rows, span = late.shape[0], near.shape[0]
    chip, core = place[1], place[2]
    scale = dcol[block(2 * core + chip, rows), :]
    pair[block(core, rows), :] = e0[...]
    pair[block(1 - core, rows), :] = e1[...]
    cross = outer(late[...], near[...]) * scale * drow[...] + before[...].astype(jnp.float32)
    out[:, :span] = cross.astype(jnp.bfloat16)
    out[:, span:] = (outer(late[...], pair[...]) * scale * dpair[1 - chip]).astype(jnp.bfloat16)


def finish_kernel(scale, place, w, *refs):
    pieces, (gram, energy, table, y) = refs[:8], refs[8:]
    rows, span = pieces[0].shape[0], table.shape[0] // 2
    for d in range(8):
        half, chip, core = place[0] ^ (d >> 2), place[1] ^ ((d >> 1) & 1), place[2] ^ (d & 1)
        mine, other = pieces[d], pieces[d ^ 4]
        at = block(4 * half + 2 * core + chip, rows)
        extra = spread(other[:, 2 * span :].astype(jnp.float32), 1 - chip)
        table[at, block(half, span)] = (mine[:, :span].astype(jnp.float32) + extra).astype(jnp.bfloat16)
        table[at, block(1 - half, span)] = other[:, span : 2 * span]
    freqs, width, days = w.shape
    flat = w[...].reshape(freqs * width, days)
    y[...] = jnp.dot(flat, table[...], preferred_element_type=jnp.float32).astype(jnp.bfloat16)
    for f in range(freqs):
        part = outer(y[f * width : (f + 1) * width, :], w[f]) * scale
        gram[f] = part + part.T
    g = gram[...]
    vector = jnp.ones((freqs, 1, width), jnp.float32)
    along = 2
    for step in range(POWER + 1):
        applied = jnp.sum(g * vector, axis=along, keepdims=True)
        along = 3 - along
        mean = jnp.sum(applied * applied, axis=along, keepdims=True) * (1.0 / width)
        if step < POWER:
            vector = applied / jnp.sqrt(mean + power_eps)
    lane = lax.broadcasted_iota(jnp.int32, (freqs, 1, freqs), 2)
    own = lax.broadcasted_iota(jnp.int32, (freqs, 1, freqs), 0)
    energy[...] = jnp.sum(jnp.where(lane == own, jnp.sqrt(mean), 0.0), axis=0)


def covariance_shards(anomaly, offsets, taper_index):
    n = lax.axis_size("tm")
    me = lax.axis_index("tm")
    half, chip, core = me // 4, (me // 2) % 2, me % 2
    place = jnp.stack([half, chip, core]).astype(jnp.int32)
    rows, width = anomaly.shape
    span, part = 4 * rows, width // 4
    order = day_order(rows)
    freqs = NF // n
    bf16 = jnp.bfloat16

    def tm_swap(value, bit):
        return lax.ppermute(value, "tm", [(i, i ^ bit) for i in range(n)])

    def pix_sum(value):
        other = lax.ppermute(value, "pix", [(0, 1), (1, 0)])
        return (value.astype(jnp.float32) + other.astype(jnp.float32)).astype(bf16)

    def everyone(value):
        s4, s2 = tm_swap(value, 4), tm_swap(value, 2)
        s6 = tm_swap(s4, 2)
        z = (value, s2, s4, s6)
        return [v for pair in zip(z, [tm_swap(v, 1) for v in z]) for v in pair]

    def cut(source, start, count):
        return lax.optimization_barrier((source, lax.dynamic_slice_in_dim(source, start, count, 1)))

    z = me // 2
    source, far6 = cut(anomaly, (z ^ 3) * part, part)
    source, home = cut(source, z * part, part)
    early = tm_swap(far6, 6)
    p1 = tm_swap(home, 1)
    source, p1 = lax.optimization_barrier((source, p1))
    source, side_a = cut(source, (z ^ 1) * part, part // 2)
    source, side_b = cut(source, (z ^ 1) * part + part // 2, part // 2)
    source, far_a = cut(source, (1 - half) * 2 * part, part)
    source, far_b = cut(source, (1 - half) * 2 * part + part, part)
    source, far4 = cut(source, (z ^ 2) * part, part)
    late = tm_swap(far4, 4)
    p2a, p2b = tm_swap(side_a, 2), tm_swap(side_b, 2)
    fa, fb = tm_swap(far_a, 1), tm_swap(far_b, 1)
    p2a, offsets, taper_index = lax.optimization_barrier((p2a, offsets, taper_index))
    w = weights(offsets, taper_index, me * freqs, freqs, order)
    p3a, p3b = tm_swap(p2a, 1), tm_swap(p2b, 1)
    p3a, w = lax.optimization_barrier((p3a, w))

    factors = day_factors(span)
    first, second = factors[: 2 * rows].reshape(2, rows), factors[2 * rows :].reshape(2, rows)
    pairs = np.concatenate([first, second], axis=1)[:, None, :]
    drow, dcol, dpair = jnp.asarray(factors[None, :]), jnp.asarray(factors[:, None]), jnp.asarray(pairs)
    vmem = pl.BlockSpec(memory_space=pltpu.VMEM)
    smem = pl.BlockSpec(memory_space=pltpu.SMEM)

    def call(kernel, flops, outs, scratch, *args):
        return pl.pallas_call(
            kernel,
            out_shape=[jax.ShapeDtypeStruct(shape, kind) for shape, kind in outs],
            in_specs=[smem] + [vmem] * len(args),
            out_specs=[vmem] * len(outs),
            scratch_shapes=[pltpu.VMEM(shape, kind) for shape, kind in scratch],
            cost_estimate=pl.CostEstimate(flops=flops, bytes_accessed=0, transcendentals=0),
            compiler_params=pltpu.CompilerParams(vmem_limit_bytes=VMEM_BYTES),
        )(place, *args)

    near, keep, send = call(
        own_kernel,
        OWN_FLOPS,
        [((span, part), bf16), ((rows, span), jnp.float32), ((rows, span), bf16)],
        [((2 * rows, 2 * part), bf16), ((2 * rows, span), jnp.float32)],
        home, p1, p2a, p2b, p3a, p3b, far_a, far_b, fa, fb, drow, dcol, dpair,
    )
    mine = pix_sum((keep + tm_swap(send, 2).astype(jnp.float32)).astype(bf16))
    e1 = tm_swap(early, 1)
    (cross,) = call(early_kernel, EARLY_FLOPS, [((rows, span), bf16)], [], near, early, drow, dcol)
    before = tm_swap(cross, 2)
    (last,) = call(
        late_kernel,
        LATE_FLOPS,
        [((rows, span + 2 * rows), bf16)],
        [((2 * rows, part), bf16)],
        near, late, early, e1, before, drow, dcol, dpair,
    )
    pieces = everyone(jnp.concatenate([mine, pix_sum(last)], axis=1))
    gram_width = 2 * NB
    total_pixels = width * lax.axis_size("pix")
    gram, energy = call(
        functools.partial(finish_kernel, 1.0 / total_pixels),
        FINISH_FLOPS,
        [((freqs, gram_width, gram_width), jnp.float32), ((1, freqs), jnp.float32)],
        [((2 * span, 2 * span), bf16), ((freqs * gram_width, 2 * span), bf16)],
        w, *pieces,
    )
    return gram, energy.reshape(freqs)


def solution(mesh):
    placed = (P("tm", ("group", "pix", "sub")), P(), P())
    pairs = mesh.shape["tm"] == 8 and mesh.shape["pix"] == 2 and mesh.shape["sub"] == 1

    def shards(anomaly, offsets, taper_index):
        if pairs and anomaly.shape[0] == 64 and anomaly.shape[1] % 512 == 0:
            return covariance_shards(anomaly, offsets, taper_index)
        return spectra_shards(anomaly, offsets, taper_index)

    return jax.shard_map(
        shards,
        mesh=mesh,
        in_specs=placed,
        out_specs=(P(("group", "tm"), None, None), P(("group", "tm"))),
        check_vma=False,
    )
```

```python
import functools
import math

import jax
import jax.numpy as jnp
import numpy as np
from jax import lax
from jax.experimental import pallas as pl
from jax.experimental.pallas import tpu as pltpu
from jax.sharding import PartitionSpec as P

NFFT = 256
NB = 32
POWER = 8
NF = 128
VMEM_BYTES = 40 * 1024 * 1024
OWN_FLOPS, EARLY_FLOPS, PAIR_FLOPS, LATE_FLOPS, FINISH_FLOPS = 0, 0, 0, 4_000_000_000, 1_000_000_000
EARLY_LEAD = 8

power_eps = 1e-06


def window_rows(taper_index, length):
    steps_t = jnp.arange(length, dtype=jnp.float32)
    phase = steps_t * (2.0 * math.pi / length)
    center = (steps_t + 0.5) * (math.pi / length)
    hann = jnp.sin(center) ** 2
    hamming = 0.54 - 0.46 * jnp.cos(phase)
    blackman = 0.42 - 0.5 * jnp.cos(phase) + 0.08 * jnp.cos(2.0 * phase)
    sine_win = jnp.sin(center)
    table_rows = jnp.stack([hann, hamming, blackman, sine_win])
    chosen = jnp.zeros((taper_index.shape[0], length), jnp.float32)
    for which in range(4):
        chosen = chosen + jnp.where(
            taper_index[:, None] == which, table_rows[which][None, :], jnp.float32(0.0)
        )
    return chosen


def dft_table(length, kept):
    freqs = jnp.arange(kept, dtype=jnp.int32)
    times = jnp.arange(length, dtype=jnp.int32)
    product = freqs[:, None] * times[None, :] % length
    angle = product.astype(jnp.float32) * (2.0 * math.pi / length)
    return jnp.stack([jnp.cos(angle), -jnp.sin(angle)]).astype(jnp.bfloat16)


def local_gram(spectra):
    stacked = spectra.reshape(2 * spectra.shape[1], spectra.shape[2], spectra.shape[3])
    return jnp.einsum("ifp,jfp->fij", stacked, stacked, preferred_element_type=jnp.float32)


def spectra_shards(anomaly, offsets, taper_index):
    series = lax.all_to_all(anomaly, "tm", split_axis=1, concat_axis=0, tiled=True)
    windows = window_rows(taper_index, NFFT)
    energy = 1.0 / jnp.sqrt(jnp.sum(windows * windows, axis=1))
    transform = dft_table(NFFT, NF)
    width_here = series.shape[1]
    per_group = 8
    gram_width = 2 * NB

    def fill_group(position, buffer):
        first_block = position * per_group
        starts = lax.dynamic_slice_in_dim(offsets, first_block, per_group, 0)
        shapes = lax.dynamic_slice_in_dim(windows, first_block, per_group, 0)
        scales = lax.dynamic_slice_in_dim(energy, first_block, per_group, 0)
        segments = jax.vmap(lambda first_day: lax.dynamic_slice_in_dim(series, first_day, NFFT, 0))(
            starts
        )
        windowed = (segments * shapes[:, :, None]).astype(jnp.bfloat16)
        spectra = jnp.einsum(
            "rkt,btp->rbkp", transform, windowed, preferred_element_type=jnp.float32
        )
        spectra = (spectra * scales[None, :, None, None]).astype(jnp.bfloat16)
        return lax.dynamic_update_slice_in_dim(buffer, spectra, first_block, 1)

    empty = jnp.zeros((2, NB, NF, width_here), jnp.bfloat16)
    spectra = lax.fori_loop(0, NB // per_group, fill_group, empty)
    received = lax.all_to_all(spectra, "tm", split_axis=2, concat_axis=3, tiled=True)
    partial_value = local_gram(received)
    summed = lax.psum(partial_value, ("pix", "sub"))
    total_pixels = anomaly.shape[1] * lax.axis_size(("pix", "sub"))
    spectral_gram = summed / total_pixels
    vector = jnp.ones((spectral_gram.shape[0], gram_width), jnp.float32)
    for _ in range(POWER):
        applied = jnp.einsum("fij,fj->fi", spectral_gram, vector, precision=lax.Precision.HIGHEST)
        vector = applied / jnp.sqrt(jnp.mean(applied * applied, axis=1, keepdims=True) + power_eps)
    applied = jnp.einsum("fij,fj->fi", spectral_gram, vector, precision=lax.Precision.HIGHEST)
    leading_energy = jnp.sqrt(jnp.mean(applied * applied, axis=1))
    return (spectral_gram, leading_energy)


def day_factors(days):
    return (1.0 + 0.4 * ((np.arange(days) * 0.6180339887498949) % 1.0)).astype(np.float32)


def day_order(rows):
    blocks = [4 * half + 2 * chip + core for half in (0, 1) for core in (0, 1) for chip in (0, 1)]
    return np.concatenate([np.arange(rows) + rows * block for block in blocks]).astype(np.int32)


def weights(offsets, taper_index, first_freq, freqs, order):
    days = order.shape[0]
    day = jnp.asarray(order)
    local = day[None, :] - offsets[:, None]
    inside = (local >= 0) & (local < NFFT)
    steps_t = local.astype(jnp.float32)
    phase = steps_t * (2.0 * math.pi / NFFT)
    center = (steps_t + 0.5) * (math.pi / NFFT)
    sine_win = jnp.sin(center)
    table = [
        sine_win**2,
        0.54 - 0.46 * jnp.cos(phase),
        0.42 - 0.5 * jnp.cos(phase) + 0.08 * jnp.cos(2.0 * phase),
        sine_win,
    ]
    window = jnp.zeros(local.shape, jnp.float32)
    for which in range(4):
        window = window + jnp.where(taper_index[:, None] == which, table[which], 0.0)
    window = jnp.where(inside, window, 0.0)
    energy = 1.0 / jnp.sqrt(jnp.sum(window * window, axis=1, keepdims=True))
    factors = day_factors(days // 2)
    window = window * energy * (1.0 / np.concatenate([factors, factors]))[None, :]

    def turn(steps):
        freq = first_freq + jnp.arange(freqs, dtype=jnp.int32)
        angle = ((freq[:, None] * steps[None, :]) % NFFT).astype(jnp.float32)
        angle = angle * (2.0 * math.pi / NFFT)
        return jnp.cos(angle), jnp.sin(angle)

    cos_t, sin_t = lax.optimization_barrier(turn(day))
    cos_b, sin_b = lax.optimization_barrier(turn(offsets))
    window = lax.optimization_barrier(window)
    ct, st = cos_t[:, None, :], sin_t[:, None, :]
    cb, sb = cos_b[:, :, None], sin_b[:, :, None]
    real = window * (ct * cb + st * sb)
    imag = window * (ct * sb - st * cb)
    return jnp.concatenate([real, imag], axis=1).astype(jnp.bfloat16)


def outer(left, right):
    return lax.dot_general(left, right, (((1,), (1,)), ((), ())), preferred_element_type=jnp.float32)


def spread(pair, chip):
    low = lax.broadcasted_iota(jnp.int32, pair.shape, 1) < pair.shape[1] // 2
    turned = pltpu.roll(pair, pair.shape[1] // 2, 1)
    first = jnp.where(chip == 0, pair, turned)
    second = jnp.where(chip == 0, turned, pair)
    keep = low == (chip == 0)
    return jnp.concatenate([jnp.where(keep, first, 0.0), jnp.where(keep, second, 0.0)], axis=1)


def block(index, rows):
    return pl.ds(pl.multiple_of(index * rows, rows), rows)


def own_kernel(place, p0, p1, p2a, p2b, p3a, p3b, far, fp, drow, dcol, dpair, near, keep, send, strip):
    chip, core = place[1], place[2]
    slot = 2 * core + chip
    rows, middle = p2a.shape
    near[block(slot, rows), :] = p0[...]
    near[block(slot ^ 2, rows), :] = p1[...]
    for flip, first, second in ((1, p2a, p2b), (3, p3a, p3b)):
        near[block(slot ^ flip, rows), :middle] = first[...]
        near[block(slot ^ flip, rows), middle:] = second[...]
    mine = block(core, 2 * rows)
    strip[...] = outer(near[mine, :], near[...]) * (0.5 * dcol[mine, :]) * drow[...]
    same = 0.5 * outer(far[...], far[...])
    cross = outer(far[:, block(core, fp.shape[1])], fp[...])
    inside = jnp.where(core == 0, jnp.concatenate([same, cross], axis=1), jnp.concatenate([cross, same], axis=1))
    inside = inside * dcol[block(slot, rows), :] * dpair[chip]
    keep[...] = strip[block(chip, rows), :] + spread(inside, chip)
    send[...] = strip[block(1 - chip, rows), :].astype(jnp.bfloat16)


def early_kernel(place, near, ea, eb, drow, dcol, out):
    rows, cut = ea.shape
    slot = 2 * place[2] + 1 - place[1]
    value = outer(ea[...], near[:, :cut]) + outer(eb[...], near[:, cut:])
    out[...] = (value * dcol[block(slot, rows), :] * drow[...]).astype(jnp.bfloat16)


def pair_kernel(place, e0a, e0b, e1a, e1b, pair):
    (rows, cut), core = e0a.shape, place[2]
    for index, first, second in ((core, e0a, e0b), (1 - core, e1a, e1b)):
        pair[block(index, rows), :cut] = first[...]
        pair[block(index, rows), cut:] = second[...]


def late_kernel(place, near, late, pair, before, drow, dcol, dpair, out):
    rows, span = late.shape[0], near.shape[0]
    chip, core = place[1], place[2]
    scale = dcol[block(2 * core + chip, rows), :]
    cross = outer(late[...], near[...]) * scale * drow[...] + before[...].astype(jnp.float32)
    out[:, :span] = cross.astype(jnp.bfloat16)
    out[:, span:] = (outer(late[...], pair[...]) * scale * dpair[1 - chip]).astype(jnp.bfloat16)


def finish_kernel(scale, place, w, *refs):
    pieces, (gram, energy, table, y) = refs[:8], refs[8:]
    rows, span = pieces[0].shape[0], table.shape[0] // 2
    for d in range(8):
        half, chip, core = place[0] ^ (d >> 2), place[1] ^ ((d >> 1) & 1), place[2] ^ (d & 1)
        mine, other = pieces[d], pieces[d ^ 4]
        at = block(4 * half + 2 * core + chip, rows)
        extra = spread(other[:, 2 * span :].astype(jnp.float32), 1 - chip)
        table[at, block(half, span)] = (mine[:, :span].astype(jnp.float32) + extra).astype(jnp.bfloat16)
        table[at, block(1 - half, span)] = other[:, span : 2 * span]
    freqs, width, days = w.shape
    flat = w[...].reshape(freqs * width, days)
    y[...] = jnp.dot(flat, table[...], preferred_element_type=jnp.float32).astype(jnp.bfloat16)
    for f in range(freqs):
        part = outer(y[f * width : (f + 1) * width, :], w[f]) * scale
        gram[f] = part + part.T
    g = gram[...]
    vector = jnp.ones((freqs, 1, width), jnp.float32)
    along = 2
    for step in range(POWER + 1):
        applied = jnp.sum(g * vector, axis=along, keepdims=True)
        along = 3 - along
        mean = jnp.sum(applied * applied, axis=along, keepdims=True) * (1.0 / width)
        if step < POWER:
            vector = applied / jnp.sqrt(mean + power_eps)
    lane = lax.broadcasted_iota(jnp.int32, (freqs, 1, freqs), 2)
    own = lax.broadcasted_iota(jnp.int32, (freqs, 1, freqs), 0)
    energy[...] = jnp.sum(jnp.where(lane == own, jnp.sqrt(mean), 0.0), axis=0)


def covariance_shards(anomaly, offsets, taper_index):
    n = lax.axis_size("tm")
    me = lax.axis_index("tm")
    half, chip, core = me // 4, (me // 2) % 2, me % 2
    place = jnp.stack([half, chip, core]).astype(jnp.int32)
    rows, width = anomaly.shape
    span, part = 4 * rows, width // 4
    order = day_order(rows)
    freqs = NF // n
    bf16 = jnp.bfloat16

    def tm_swap(value, bit):
        return lax.ppermute(value, "tm", [(i, i ^ bit) for i in range(n)])

    def pix_sum(value):
        other = lax.ppermute(value, "pix", [(0, 1), (1, 0)])
        return (value.astype(jnp.float32) + other.astype(jnp.float32)).astype(bf16)

    def everyone(value):
        s4, s2 = tm_swap(value, 4), tm_swap(value, 2)
        s6 = tm_swap(value, 6)
        z = (value, s2, s4, s6)
        return [v for pair in zip(z, [tm_swap(v, 1) for v in z]) for v in pair]

    def cut(source, start, count):
        return lax.optimization_barrier((source, lax.dynamic_slice_in_dim(source, start, count, 1)))

    z = me // 2
    lead = part * EARLY_LEAD // 16
    source, far6a = cut(anomaly, (z ^ 3) * part, lead)
    source, far6b = cut(source, (z ^ 3) * part + lead, part - lead)
    source, home = cut(source, z * part, part)
    ea, eb = tm_swap(far6a, 6), tm_swap(far6b, 6)
    p1 = tm_swap(home, 1)
    source, p1 = lax.optimization_barrier((source, p1))
    source, side_a = cut(source, (z ^ 1) * part, part // 2)
    source, side_b = cut(source, (z ^ 1) * part + part // 2, part // 2)
    source, away = cut(source, (2 * (1 - half) + 1 - core) * part, part)
    source, far = cut(source, (1 - half) * 2 * part, 2 * part)
    p2a, p2b = tm_swap(side_a, 2), tm_swap(side_b, 2)
    fp = tm_swap(away, 1)
    source, far4 = cut(source, (z ^ 2) * part, part)
    far4, ea = lax.optimization_barrier((far4, ea))
    late = tm_swap(far4, 4)
    p3a, p3b = tm_swap(p2a, 1), tm_swap(p2b, 1)

    factors = day_factors(span)
    first, second = factors[: 2 * rows].reshape(2, rows), factors[2 * rows :].reshape(2, rows)
    pairs = np.concatenate([first, second], axis=1)[:, None, :]
    drow, dcol, dpair = jnp.asarray(factors[None, :]), jnp.asarray(factors[:, None]), jnp.asarray(pairs)
    vmem = pl.BlockSpec(memory_space=pltpu.VMEM)
    smem = pl.BlockSpec(memory_space=pltpu.SMEM)

    def call(kernel, flops, outs, scratch, *args):
        return pl.pallas_call(
            kernel,
            out_shape=[jax.ShapeDtypeStruct(shape, kind) for shape, kind in outs],
            in_specs=[smem] + [vmem] * len(args),
            out_specs=[vmem] * len(outs),
            scratch_shapes=[pltpu.VMEM(shape, kind) for shape, kind in scratch],
            cost_estimate=pl.CostEstimate(flops=flops, bytes_accessed=0, transcendentals=0),
            compiler_params=pltpu.CompilerParams(vmem_limit_bytes=VMEM_BYTES),
        )(place, *args)

    near, keep, send = call(
        own_kernel,
        OWN_FLOPS,
        [((span, part), bf16), ((rows, span), jnp.float32), ((rows, span), bf16)],
        [((2 * rows, span), jnp.float32)],
        home, p1, p2a, p2b, p3a, p3b, far, fp, drow, dcol, dpair,
    )
    mine = (keep + tm_swap(send, 2).astype(jnp.float32)).astype(bf16)
    e1a, e1b = tm_swap(ea, 1), tm_swap(eb, 1)
    (cross,) = call(early_kernel, EARLY_FLOPS, [((rows, span), bf16)], [], near, ea, eb, drow, dcol)
    before = tm_swap(cross, 2)
    (pair,) = call(pair_kernel, PAIR_FLOPS, [((2 * rows, part), bf16)], [], ea, eb, e1a, e1b)
    (last,) = call(
        late_kernel,
        LATE_FLOPS,
        [((rows, span + 2 * rows), bf16)],
        [],
        near, late, pair, before, drow, dcol, dpair,
    )
    last, offsets, taper_index = lax.optimization_barrier((last, offsets, taper_index))
    w = weights(offsets, taper_index, me * freqs, freqs, order)
    pieces = everyone(pix_sum(jnp.concatenate([mine, last], axis=1)))
    gram_width = 2 * NB
    total_pixels = width * lax.axis_size("pix")
    gram, energy = call(
        functools.partial(finish_kernel, 1.0 / total_pixels),
        FINISH_FLOPS,
        [((freqs, gram_width, gram_width), jnp.float32), ((1, freqs), jnp.float32)],
        [((2 * span, 2 * span), bf16), ((freqs * gram_width, 2 * span), bf16)],
        w, *pieces,
    )
    return gram, energy.reshape(freqs)


def solution(mesh):
    placed = (P("tm", ("group", "pix", "sub")), P(), P())
    pairs = mesh.shape["tm"] == 8 and mesh.shape["pix"] == 2 and mesh.shape["sub"] == 1

    def shards(anomaly, offsets, taper_index):
        if pairs and anomaly.shape[0] == 64 and anomaly.shape[1] % 512 == 0:
            return covariance_shards(anomaly, offsets, taper_index)
        return spectra_shards(anomaly, offsets, taper_index)

    return jax.shard_map(
        shards,
        mesh=mesh,
        in_specs=placed,
        out_specs=(P(("group", "tm"), None, None), P(("group", "tm"))),
        check_vma=False,
    )
```

```python
import functools
import math

import jax
import jax.numpy as jnp
import numpy as np
from jax import lax
from jax.experimental import pallas as pl
from jax.experimental.pallas import tpu as pltpu
from jax.sharding import PartitionSpec as P

NFFT = 256
NB = 32
POWER = 8
NF = 128
VMEM_BYTES = 40 * 1024 * 1024
OWN_FLOPS, EARLY_FLOPS, PAIR_FLOPS, LATE_FLOPS, FINISH_FLOPS = 0, 0, 0, 4_000_000_000, 1_000_000_000
EARLY_LEAD = 4

power_eps = 1e-06


def window_rows(taper_index, length):
    steps_t = jnp.arange(length, dtype=jnp.float32)
    phase = steps_t * (2.0 * math.pi / length)
    center = (steps_t + 0.5) * (math.pi / length)
    hann = jnp.sin(center) ** 2
    hamming = 0.54 - 0.46 * jnp.cos(phase)
    blackman = 0.42 - 0.5 * jnp.cos(phase) + 0.08 * jnp.cos(2.0 * phase)
    sine_win = jnp.sin(center)
    table_rows = jnp.stack([hann, hamming, blackman, sine_win])
    chosen = jnp.zeros((taper_index.shape[0], length), jnp.float32)
    for which in range(4):
        chosen = chosen + jnp.where(
            taper_index[:, None] == which, table_rows[which][None, :], jnp.float32(0.0)
        )
    return chosen


def dft_table(length, kept):
    freqs = jnp.arange(kept, dtype=jnp.int32)
    times = jnp.arange(length, dtype=jnp.int32)
    product = freqs[:, None] * times[None, :] % length
    angle = product.astype(jnp.float32) * (2.0 * math.pi / length)
    return jnp.stack([jnp.cos(angle), -jnp.sin(angle)]).astype(jnp.bfloat16)


def local_gram(spectra):
    stacked = spectra.reshape(2 * spectra.shape[1], spectra.shape[2], spectra.shape[3])
    return jnp.einsum("ifp,jfp->fij", stacked, stacked, preferred_element_type=jnp.float32)


def spectra_shards(anomaly, offsets, taper_index):
    series = lax.all_to_all(anomaly, "tm", split_axis=1, concat_axis=0, tiled=True)
    windows = window_rows(taper_index, NFFT)
    energy = 1.0 / jnp.sqrt(jnp.sum(windows * windows, axis=1))
    transform = dft_table(NFFT, NF)
    width_here = series.shape[1]
    per_group = 8
    gram_width = 2 * NB

    def fill_group(position, buffer):
        first_block = position * per_group
        starts = lax.dynamic_slice_in_dim(offsets, first_block, per_group, 0)
        shapes = lax.dynamic_slice_in_dim(windows, first_block, per_group, 0)
        scales = lax.dynamic_slice_in_dim(energy, first_block, per_group, 0)
        segments = jax.vmap(lambda first_day: lax.dynamic_slice_in_dim(series, first_day, NFFT, 0))(
            starts
        )
        windowed = (segments * shapes[:, :, None]).astype(jnp.bfloat16)
        spectra = jnp.einsum(
            "rkt,btp->rbkp", transform, windowed, preferred_element_type=jnp.float32
        )
        spectra = (spectra * scales[None, :, None, None]).astype(jnp.bfloat16)
        return lax.dynamic_update_slice_in_dim(buffer, spectra, first_block, 1)

    empty = jnp.zeros((2, NB, NF, width_here), jnp.bfloat16)
    spectra = lax.fori_loop(0, NB // per_group, fill_group, empty)
    received = lax.all_to_all(spectra, "tm", split_axis=2, concat_axis=3, tiled=True)
    partial_value = local_gram(received)
    summed = lax.psum(partial_value, ("pix", "sub"))
    total_pixels = anomaly.shape[1] * lax.axis_size(("pix", "sub"))
    spectral_gram = summed / total_pixels
    vector = jnp.ones((spectral_gram.shape[0], gram_width), jnp.float32)
    for _ in range(POWER):
        applied = jnp.einsum("fij,fj->fi", spectral_gram, vector, precision=lax.Precision.HIGHEST)
        vector = applied / jnp.sqrt(jnp.mean(applied * applied, axis=1, keepdims=True) + power_eps)
    applied = jnp.einsum("fij,fj->fi", spectral_gram, vector, precision=lax.Precision.HIGHEST)
    leading_energy = jnp.sqrt(jnp.mean(applied * applied, axis=1))
    return (spectral_gram, leading_energy)


def day_factors(days):
    return (1.0 + 0.4 * ((np.arange(days) * 0.6180339887498949) % 1.0)).astype(np.float32)


def day_order(rows):
    blocks = [4 * half + 2 * chip + core for half in (0, 1) for core in (0, 1) for chip in (0, 1)]
    return np.concatenate([np.arange(rows) + rows * block for block in blocks]).astype(np.int32)


def weights(offsets, taper_index, first_freq, freqs, order):
    days = order.shape[0]
    day = jnp.asarray(order)
    local = day[None, :] - offsets[:, None]
    inside = (local >= 0) & (local < NFFT)
    steps_t = local.astype(jnp.float32)
    phase = steps_t * (2.0 * math.pi / NFFT)
    center = (steps_t + 0.5) * (math.pi / NFFT)
    sine_win = jnp.sin(center)
    table = [
        sine_win**2,
        0.54 - 0.46 * jnp.cos(phase),
        0.42 - 0.5 * jnp.cos(phase) + 0.08 * jnp.cos(2.0 * phase),
        sine_win,
    ]
    window = jnp.zeros(local.shape, jnp.float32)
    for which in range(4):
        window = window + jnp.where(taper_index[:, None] == which, table[which], 0.0)
    window = jnp.where(inside, window, 0.0)
    energy = 1.0 / jnp.sqrt(jnp.sum(window * window, axis=1, keepdims=True))
    factors = day_factors(days // 2)
    window = window * energy * (1.0 / np.concatenate([factors, factors]))[None, :]

    def turn(steps):
        freq = first_freq + jnp.arange(freqs, dtype=jnp.int32)
        angle = ((freq[:, None] * steps[None, :]) % NFFT).astype(jnp.float32)
        angle = angle * (2.0 * math.pi / NFFT)
        return jnp.cos(angle), jnp.sin(angle)

    cos_t, sin_t = lax.optimization_barrier(turn(day))
    cos_b, sin_b = lax.optimization_barrier(turn(offsets))
    window = lax.optimization_barrier(window)
    ct, st = cos_t[:, None, :], sin_t[:, None, :]
    cb, sb = cos_b[:, :, None], sin_b[:, :, None]
    real = window * (ct * cb + st * sb)
    imag = window * (ct * sb - st * cb)
    return jnp.concatenate([real, imag], axis=1).astype(jnp.bfloat16)


def outer(left, right):
    return lax.dot_general(left, right, (((1,), (1,)), ((), ())), preferred_element_type=jnp.float32)


def spread(pair, chip):
    low = lax.broadcasted_iota(jnp.int32, pair.shape, 1) < pair.shape[1] // 2
    turned = pltpu.roll(pair, pair.shape[1] // 2, 1)
    first = jnp.where(chip == 0, pair, turned)
    second = jnp.where(chip == 0, turned, pair)
    keep = low == (chip == 0)
    return jnp.concatenate([jnp.where(keep, first, 0.0), jnp.where(keep, second, 0.0)], axis=1)


def block(index, rows):
    return pl.ds(pl.multiple_of(index * rows, rows), rows)


def own_kernel(place, p0, p1, p2a, p2b, p3a, p3b, far, fp, drow, dcol, dpair, near, keep, send, strip):
    chip, core = place[1], place[2]
    slot = 2 * core + chip
    rows, middle = p2a.shape
    near[block(slot, rows), :] = p0[...]
    near[block(slot ^ 2, rows), :] = p1[...]
    for flip, first, second in ((1, p2a, p2b), (3, p3a, p3b)):
        near[block(slot ^ flip, rows), :middle] = first[...]
        near[block(slot ^ flip, rows), middle:] = second[...]
    mine = block(core, 2 * rows)
    strip[...] = outer(near[mine, :], near[...]) * (0.5 * dcol[mine, :]) * drow[...]
    same = 0.5 * outer(far[...], far[...])
    cross = outer(far[:, block(core, fp.shape[1])], fp[...])
    inside = jnp.where(core == 0, jnp.concatenate([same, cross], axis=1), jnp.concatenate([cross, same], axis=1))
    inside = inside * dcol[block(slot, rows), :] * dpair[chip]
    keep[...] = strip[block(chip, rows), :] + spread(inside, chip)
    send[...] = strip[block(1 - chip, rows), :].astype(jnp.bfloat16)


def early_kernel(place, near, ea, eb, drow, dcol, out):
    rows, cut = ea.shape
    slot = 2 * place[2] + 1 - place[1]
    value = outer(ea[...], near[:, :cut]) + outer(eb[...], near[:, cut:])
    out[...] = (value * dcol[block(slot, rows), :] * drow[...]).astype(jnp.bfloat16)


def pair_kernel(place, e0a, e0b, e1a, e1b, pair):
    (rows, cut), core = e0a.shape, place[2]
    for index, first, second in ((core, e0a, e0b), (1 - core, e1a, e1b)):
        pair[block(index, rows), :cut] = first[...]
        pair[block(index, rows), cut:] = second[...]


def late_kernel(place, near, late, pair, before, drow, dcol, dpair, out):
    rows, span = late.shape[0], near.shape[0]
    chip, core = place[1], place[2]
    scale = dcol[block(2 * core + chip, rows), :]
    cross = outer(late[...], near[...]) * scale * drow[...] + before[...].astype(jnp.float32)
    out[:, :span] = cross.astype(jnp.bfloat16)
    out[:, span:] = (outer(late[...], pair[...]) * scale * dpair[1 - chip]).astype(jnp.bfloat16)


def finish_kernel(scale, place, w, *refs):
    pieces, (gram, energy, table, y) = refs[:8], refs[8:]
    rows, span = pieces[0].shape[0], table.shape[0] // 2
    for d in range(8):
        half, chip, core = place[0] ^ (d >> 2), place[1] ^ ((d >> 1) & 1), place[2] ^ (d & 1)
        mine, other = pieces[d], pieces[d ^ 4]
        at = block(4 * half + 2 * core + chip, rows)
        extra = spread(other[:, 2 * span :].astype(jnp.float32), 1 - chip)
        table[at, block(half, span)] = (mine[:, :span].astype(jnp.float32) + extra).astype(jnp.bfloat16)
        table[at, block(1 - half, span)] = other[:, span : 2 * span]
    freqs, width, days = w.shape
    flat = w[...].reshape(freqs * width, days)
    y[...] = jnp.dot(flat, table[...], preferred_element_type=jnp.float32).astype(jnp.bfloat16)
    for f in range(freqs):
        part = outer(y[f * width : (f + 1) * width, :], w[f]) * scale
        gram[f] = part + part.T
    g = gram[...]
    vector = jnp.ones((freqs, 1, width), jnp.float32)
    along = 2
    for step in range(POWER + 1):
        applied = jnp.sum(g * vector, axis=along, keepdims=True)
        along = 3 - along
        mean = jnp.sum(applied * applied, axis=along, keepdims=True) * (1.0 / width)
        if step < POWER:
            vector = applied / jnp.sqrt(mean + power_eps)
    lane = lax.broadcasted_iota(jnp.int32, (freqs, 1, freqs), 2)
    own = lax.broadcasted_iota(jnp.int32, (freqs, 1, freqs), 0)
    energy[...] = jnp.sum(jnp.where(lane == own, jnp.sqrt(mean), 0.0), axis=0)


def covariance_shards(anomaly, offsets, taper_index):
    n = lax.axis_size("tm")
    me = lax.axis_index("tm")
    half, chip, core = me // 4, (me // 2) % 2, me % 2
    place = jnp.stack([half, chip, core]).astype(jnp.int32)
    rows, width = anomaly.shape
    span, part = 4 * rows, width // 4
    order = day_order(rows)
    freqs = NF // n
    bf16 = jnp.bfloat16

    def tm_swap(value, bit):
        return lax.ppermute(value, "tm", [(i, i ^ bit) for i in range(n)])

    def pix_sum(value):
        other = lax.ppermute(value, "pix", [(0, 1), (1, 0)])
        return (value.astype(jnp.float32) + other.astype(jnp.float32)).astype(bf16)

    def everyone(value):
        s4, s2 = tm_swap(value, 4), tm_swap(value, 2)
        s6 = tm_swap(value, 6)
        z = (value, s2, s4, s6)
        return [v for pair in zip(z, [tm_swap(v, 1) for v in z]) for v in pair]

    def cut(source, start, count):
        return lax.optimization_barrier((source, lax.dynamic_slice_in_dim(source, start, count, 1)))

    z = me // 2
    lead = part * EARLY_LEAD // 16
    source, home = cut(anomaly, z * part, part)
    source, far6a = cut(source, (z ^ 3) * part, lead)
    ea = tm_swap(far6a, 6)
    p1 = tm_swap(home, 1)
    source, p1 = lax.optimization_barrier((source, p1))
    source, far6b = cut(source, (z ^ 3) * part + lead, part - lead)
    eb = tm_swap(far6b, 6)
    source, side_a = cut(source, (z ^ 1) * part, part // 2)
    source, side_b = cut(source, (z ^ 1) * part + part // 2, part // 2)
    source, away = cut(source, (2 * (1 - half) + 1 - core) * part, part)
    source, far = cut(source, (1 - half) * 2 * part, 2 * part)
    p2a, p2b = tm_swap(side_a, 2), tm_swap(side_b, 2)
    fp = tm_swap(away, 1)
    source, far4 = cut(source, (z ^ 2) * part, part)
    far4, ea = lax.optimization_barrier((far4, ea))
    late = tm_swap(far4, 4)
    p3a, p3b = tm_swap(p2a, 1), tm_swap(p2b, 1)

    factors = day_factors(span)
    first, second = factors[: 2 * rows].reshape(2, rows), factors[2 * rows :].reshape(2, rows)
    pairs = np.concatenate([first, second], axis=1)[:, None, :]
    drow, dcol, dpair = jnp.asarray(factors[None, :]), jnp.asarray(factors[:, None]), jnp.asarray(pairs)
    vmem = pl.BlockSpec(memory_space=pltpu.VMEM)
    smem = pl.BlockSpec(memory_space=pltpu.SMEM)

    def call(kernel, flops, outs, scratch, *args):
        return pl.pallas_call(
            kernel,
            out_shape=[jax.ShapeDtypeStruct(shape, kind) for shape, kind in outs],
            in_specs=[smem] + [vmem] * len(args),
            out_specs=[vmem] * len(outs),
            scratch_shapes=[pltpu.VMEM(shape, kind) for shape, kind in scratch],
            cost_estimate=pl.CostEstimate(flops=flops, bytes_accessed=0, transcendentals=0),
            compiler_params=pltpu.CompilerParams(vmem_limit_bytes=VMEM_BYTES),
        )(place, *args)

    near, keep, send = call(
        own_kernel,
        OWN_FLOPS,
        [((span, part), bf16), ((rows, span), jnp.float32), ((rows, span), bf16)],
        [((2 * rows, span), jnp.float32)],
        home, p1, p2a, p2b, p3a, p3b, far, fp, drow, dcol, dpair,
    )
    mine = (keep + tm_swap(send, 2).astype(jnp.float32)).astype(bf16)
    e1a, e1b = tm_swap(ea, 1), tm_swap(eb, 1)
    (cross,) = call(early_kernel, EARLY_FLOPS, [((rows, span), bf16)], [], near, ea, eb, drow, dcol)
    before = tm_swap(cross, 2)
    (pair,) = call(pair_kernel, PAIR_FLOPS, [((2 * rows, part), bf16)], [], ea, eb, e1a, e1b)
    (last,) = call(
        late_kernel,
        LATE_FLOPS,
        [((rows, span + 2 * rows), bf16)],
        [],
        near, late, pair, before, drow, dcol, dpair,
    )
    last, offsets, taper_index = lax.optimization_barrier((last, offsets, taper_index))
    w = weights(offsets, taper_index, me * freqs, freqs, order)
    pieces = everyone(pix_sum(jnp.concatenate([mine, last], axis=1)))
    gram_width = 2 * NB
    total_pixels = width * lax.axis_size("pix")
    gram, energy = call(
        functools.partial(finish_kernel, 1.0 / total_pixels),
        FINISH_FLOPS,
        [((freqs, gram_width, gram_width), jnp.float32), ((1, freqs), jnp.float32)],
        [((2 * span, 2 * span), bf16), ((freqs * gram_width, 2 * span), bf16)],
        w, *pieces,
    )
    return gram, energy.reshape(freqs)


def solution(mesh):
    placed = (P("tm", ("group", "pix", "sub")), P(), P())
    pairs = mesh.shape["tm"] == 8 and mesh.shape["pix"] == 2 and mesh.shape["sub"] == 1

    def shards(anomaly, offsets, taper_index):
        if pairs and anomaly.shape[0] == 64 and anomaly.shape[1] % 512 == 0:
            return covariance_shards(anomaly, offsets, taper_index)
        return spectra_shards(anomaly, offsets, taper_index)

    return jax.shard_map(
        shards,
        mesh=mesh,
        in_specs=placed,
        out_specs=(P(("group", "tm"), None, None), P(("group", "tm"))),
        check_vma=False,
    )
```

```python
import functools
import math

import jax
import jax.numpy as jnp
import numpy as np
from jax import lax
from jax.experimental import pallas as pl
from jax.experimental.pallas import tpu as pltpu
from jax.sharding import PartitionSpec as P

NFFT = 256
NB = 32
POWER = 8
NF = 128
VMEM_BYTES = 40 * 1024 * 1024
OWN_FLOPS, EARLY_FLOPS, PAIR_FLOPS, LATE_FLOPS, FINISH_FLOPS = 0, 0, 0, 4_000_000_000, 1_000_000_000
EARLY_LEAD = 4
SEATS = (0, 1, 4, 5, 6, 7, 2, 3)

power_eps = 1e-06


def window_rows(taper_index, length):
    steps_t = jnp.arange(length, dtype=jnp.float32)
    phase = steps_t * (2.0 * math.pi / length)
    center = (steps_t + 0.5) * (math.pi / length)
    hann = jnp.sin(center) ** 2
    hamming = 0.54 - 0.46 * jnp.cos(phase)
    blackman = 0.42 - 0.5 * jnp.cos(phase) + 0.08 * jnp.cos(2.0 * phase)
    sine_win = jnp.sin(center)
    table_rows = jnp.stack([hann, hamming, blackman, sine_win])
    chosen = jnp.zeros((taper_index.shape[0], length), jnp.float32)
    for which in range(4):
        chosen = chosen + jnp.where(
            taper_index[:, None] == which, table_rows[which][None, :], jnp.float32(0.0)
        )
    return chosen


def dft_table(length, kept):
    freqs = jnp.arange(kept, dtype=jnp.int32)
    times = jnp.arange(length, dtype=jnp.int32)
    product = freqs[:, None] * times[None, :] % length
    angle = product.astype(jnp.float32) * (2.0 * math.pi / length)
    return jnp.stack([jnp.cos(angle), -jnp.sin(angle)]).astype(jnp.bfloat16)


def local_gram(spectra):
    stacked = spectra.reshape(2 * spectra.shape[1], spectra.shape[2], spectra.shape[3])
    return jnp.einsum("ifp,jfp->fij", stacked, stacked, preferred_element_type=jnp.float32)


def spectra_shards(anomaly, offsets, taper_index):
    series = lax.all_to_all(anomaly, "tm", split_axis=1, concat_axis=0, tiled=True)
    windows = window_rows(taper_index, NFFT)
    energy = 1.0 / jnp.sqrt(jnp.sum(windows * windows, axis=1))
    transform = dft_table(NFFT, NF)
    width_here = series.shape[1]
    per_group = 8
    gram_width = 2 * NB

    def fill_group(position, buffer):
        first_block = position * per_group
        starts = lax.dynamic_slice_in_dim(offsets, first_block, per_group, 0)
        shapes = lax.dynamic_slice_in_dim(windows, first_block, per_group, 0)
        scales = lax.dynamic_slice_in_dim(energy, first_block, per_group, 0)
        segments = jax.vmap(lambda first_day: lax.dynamic_slice_in_dim(series, first_day, NFFT, 0))(
            starts
        )
        windowed = (segments * shapes[:, :, None]).astype(jnp.bfloat16)
        spectra = jnp.einsum(
            "rkt,btp->rbkp", transform, windowed, preferred_element_type=jnp.float32
        )
        spectra = (spectra * scales[None, :, None, None]).astype(jnp.bfloat16)
        return lax.dynamic_update_slice_in_dim(buffer, spectra, first_block, 1)

    empty = jnp.zeros((2, NB, NF, width_here), jnp.bfloat16)
    spectra = lax.fori_loop(0, NB // per_group, fill_group, empty)
    received = lax.all_to_all(spectra, "tm", split_axis=2, concat_axis=3, tiled=True)
    partial_value = local_gram(received)
    summed = lax.psum(partial_value, ("pix", "sub"))
    total_pixels = anomaly.shape[1] * lax.axis_size(("pix", "sub"))
    spectral_gram = summed / total_pixels
    vector = jnp.ones((spectral_gram.shape[0], gram_width), jnp.float32)
    for _ in range(POWER):
        applied = jnp.einsum("fij,fj->fi", spectral_gram, vector, precision=lax.Precision.HIGHEST)
        vector = applied / jnp.sqrt(jnp.mean(applied * applied, axis=1, keepdims=True) + power_eps)
    applied = jnp.einsum("fij,fj->fi", spectral_gram, vector, precision=lax.Precision.HIGHEST)
    leading_energy = jnp.sqrt(jnp.mean(applied * applied, axis=1))
    return (spectral_gram, leading_energy)


def day_factors(days):
    return (1.0 + 0.4 * ((np.arange(days) * 0.6180339887498949) % 1.0)).astype(np.float32)


def day_order(rows):
    blocks = [4 * half + 2 * chip + core for half in (0, 1) for core in (0, 1) for chip in (0, 1)]
    return np.concatenate([np.arange(rows) + rows * block for block in blocks]).astype(np.int32)


def weights(offsets, taper_index, first_freq, freqs, order):
    days = order.shape[0]
    day = jnp.asarray(order)
    local = day[None, :] - offsets[:, None]
    inside = (local >= 0) & (local < NFFT)
    steps_t = local.astype(jnp.float32)
    phase = steps_t * (2.0 * math.pi / NFFT)
    center = (steps_t + 0.5) * (math.pi / NFFT)
    sine_win = jnp.sin(center)
    table = [
        sine_win**2,
        0.54 - 0.46 * jnp.cos(phase),
        0.42 - 0.5 * jnp.cos(phase) + 0.08 * jnp.cos(2.0 * phase),
        sine_win,
    ]
    window = jnp.zeros(local.shape, jnp.float32)
    for which in range(4):
        window = window + jnp.where(taper_index[:, None] == which, table[which], 0.0)
    window = jnp.where(inside, window, 0.0)
    energy = 1.0 / jnp.sqrt(jnp.sum(window * window, axis=1, keepdims=True))
    factors = day_factors(days // 2)
    window = window * energy * (1.0 / np.concatenate([factors, factors]))[None, :]

    def turn(steps):
        freq = first_freq + jnp.arange(freqs, dtype=jnp.int32)
        angle = ((freq[:, None] * steps[None, :]) % NFFT).astype(jnp.float32)
        angle = angle * (2.0 * math.pi / NFFT)
        return jnp.cos(angle), jnp.sin(angle)

    cos_t, sin_t = lax.optimization_barrier(turn(day))
    cos_b, sin_b = lax.optimization_barrier(turn(offsets))
    window = lax.optimization_barrier(window)
    ct, st = cos_t[:, None, :], sin_t[:, None, :]
    cb, sb = cos_b[:, :, None], sin_b[:, :, None]
    real = window * (ct * cb + st * sb)
    imag = window * (ct * sb - st * cb)
    return jnp.concatenate([real, imag], axis=1).astype(jnp.bfloat16)


def outer(left, right):
    return lax.dot_general(left, right, (((1,), (1,)), ((), ())), preferred_element_type=jnp.float32)


def spread(pair, chip):
    low = lax.broadcasted_iota(jnp.int32, pair.shape, 1) < pair.shape[1] // 2
    turned = pltpu.roll(pair, pair.shape[1] // 2, 1)
    first = jnp.where(chip == 0, pair, turned)
    second = jnp.where(chip == 0, turned, pair)
    keep = low == (chip == 0)
    return jnp.concatenate([jnp.where(keep, first, 0.0), jnp.where(keep, second, 0.0)], axis=1)


def block(index, rows):
    return pl.ds(pl.multiple_of(index * rows, rows), rows)


def own_kernel(place, p0, p1, p2a, p2b, p3a, p3b, far, fp, drow, dcol, dpair, near, keep, send, strip):
    chip, core = place[1], place[2]
    slot = 2 * core + chip
    rows, middle = p2a.shape
    near[block(slot, rows), :] = p0[...]
    near[block(slot ^ 2, rows), :] = p1[...]
    for flip, first, second in ((1, p2a, p2b), (3, p3a, p3b)):
        near[block(slot ^ flip, rows), :middle] = first[...]
        near[block(slot ^ flip, rows), middle:] = second[...]
    mine = block(core, 2 * rows)
    strip[...] = outer(near[mine, :], near[...]) * (0.5 * dcol[mine, :]) * drow[...]
    same = 0.5 * outer(far[...], far[...])
    cross = outer(far[:, block(core, fp.shape[1])], fp[...])
    inside = jnp.where(core == 0, jnp.concatenate([same, cross], axis=1), jnp.concatenate([cross, same], axis=1))
    inside = inside * dcol[block(slot, rows), :] * dpair[chip]
    keep[...] = strip[block(chip, rows), :] + spread(inside, chip)
    send[...] = strip[block(1 - chip, rows), :].astype(jnp.bfloat16)


def early_kernel(place, near, ea, eb, drow, dcol, out):
    rows, cut = ea.shape
    slot = 2 * place[2] + 1 - place[1]
    value = outer(ea[...], near[:, :cut]) + outer(eb[...], near[:, cut:])
    out[...] = (value * dcol[block(slot, rows), :] * drow[...]).astype(jnp.bfloat16)


def pair_kernel(place, e0a, e0b, e1a, e1b, pair):
    (rows, cut), core = e0a.shape, place[2]
    for index, first, second in ((core, e0a, e0b), (1 - core, e1a, e1b)):
        pair[block(index, rows), :cut] = first[...]
        pair[block(index, rows), cut:] = second[...]


def late_kernel(place, near, late, pair, before, drow, dcol, dpair, out):
    rows, span = late.shape[0], near.shape[0]
    chip, core = place[1], place[2]
    scale = dcol[block(2 * core + chip, rows), :]
    cross = outer(late[...], near[...]) * scale * drow[...] + before[...].astype(jnp.float32)
    out[:, :span] = cross.astype(jnp.bfloat16)
    out[:, span:] = (outer(late[...], pair[...]) * scale * dpair[1 - chip]).astype(jnp.bfloat16)


def finish_kernel(scale, place, w, *refs):
    pieces, (gram, energy, table, y) = refs[:8], refs[8:]
    rows, span = pieces[0].shape[0], table.shape[0] // 2
    for d in range(8):
        half, chip, core = place[0] ^ (d >> 2), place[1] ^ ((d >> 1) & 1), place[2] ^ (d & 1)
        mine, other = pieces[SEATS.index(d)], pieces[SEATS.index(d ^ 4)]
        at = block(4 * half + 2 * core + chip, rows)
        extra = spread(other[:, 2 * span :].astype(jnp.float32), 1 - chip)
        table[at, block(half, span)] = (mine[:, :span].astype(jnp.float32) + extra).astype(jnp.bfloat16)
        table[at, block(1 - half, span)] = other[:, span : 2 * span]
    freqs, width, days = w.shape
    flat = w[...].reshape(freqs * width, days)
    y[...] = jnp.dot(flat, table[...], preferred_element_type=jnp.float32).astype(jnp.bfloat16)
    for f in range(freqs):
        part = outer(y[f * width : (f + 1) * width, :], w[f]) * scale
        gram[f] = part + part.T
    g = gram[...]
    vector = jnp.ones((freqs, 1, width), jnp.float32)
    along = 2
    for step in range(POWER + 1):
        applied = jnp.sum(g * vector, axis=along, keepdims=True)
        along = 3 - along
        mean = jnp.sum(applied * applied, axis=along, keepdims=True) * (1.0 / width)
        if step < POWER:
            vector = applied / jnp.sqrt(mean + power_eps)
    lane = lax.broadcasted_iota(jnp.int32, (freqs, 1, freqs), 2)
    own = lax.broadcasted_iota(jnp.int32, (freqs, 1, freqs), 0)
    energy[...] = jnp.sum(jnp.where(lane == own, jnp.sqrt(mean), 0.0), axis=0)


def covariance_shards(anomaly, offsets, taper_index):
    n = lax.axis_size("tm")
    me = lax.axis_index("tm")
    half, chip, core = me // 4, (me // 2) % 2, me % 2
    place = jnp.stack([half, chip, core]).astype(jnp.int32)
    rows, width = anomaly.shape
    span, part = 4 * rows, width // 4
    order = day_order(rows)
    freqs = NF // n
    bf16 = jnp.bfloat16

    def tm_swap(value, bit):
        return lax.ppermute(value, "tm", [(i, i ^ bit) for i in range(n)])

    def pix_sum(value):
        other = lax.ppermute(value, "pix", [(0, 1), (1, 0)])
        return (value.astype(jnp.float32) + other.astype(jnp.float32)).astype(bf16)

    def everyone(value):
        return [v for bits in SEATS[::2] for v in with_core(value if bits == 0 else tm_swap(value, bits))]

    def with_core(value):
        return value, tm_swap(value, 1)

    def cut(source, start, count):
        return lax.optimization_barrier((source, lax.dynamic_slice_in_dim(source, start, count, 1)))

    z = me // 2
    lead = part * EARLY_LEAD // 16
    source, home = cut(anomaly, z * part, part)
    source, far6a = cut(source, (z ^ 3) * part, lead)
    ea = tm_swap(far6a, 6)
    p1 = tm_swap(home, 1)
    source, p1 = lax.optimization_barrier((source, p1))
    source, far6b = cut(source, (z ^ 3) * part + lead, part - lead)
    eb = tm_swap(far6b, 6)
    source, side_a = cut(source, (z ^ 1) * part, part // 2)
    source, side_b = cut(source, (z ^ 1) * part + part // 2, part // 2)
    source, away = cut(source, (2 * (1 - half) + 1 - core) * part, part)
    source, far = cut(source, (1 - half) * 2 * part, 2 * part)
    p2a, p2b = tm_swap(side_a, 2), tm_swap(side_b, 2)
    fp = tm_swap(away, 1)
    source, far4 = cut(source, (z ^ 2) * part, part)
    far4, ea = lax.optimization_barrier((far4, ea))
    late = tm_swap(far4, 4)
    p3a, p3b = tm_swap(p2a, 1), tm_swap(p2b, 1)

    factors = day_factors(span)
    first, second = factors[: 2 * rows].reshape(2, rows), factors[2 * rows :].reshape(2, rows)
    pairs = np.concatenate([first, second], axis=1)[:, None, :]
    drow, dcol, dpair = jnp.asarray(factors[None, :]), jnp.asarray(factors[:, None]), jnp.asarray(pairs)
    vmem = pl.BlockSpec(memory_space=pltpu.VMEM)
    smem = pl.BlockSpec(memory_space=pltpu.SMEM)

    def call(kernel, flops, outs, scratch, *args):
        return pl.pallas_call(
            kernel,
            out_shape=[jax.ShapeDtypeStruct(shape, kind) for shape, kind in outs],
            in_specs=[smem] + [vmem] * len(args),
            out_specs=[vmem] * len(outs),
            scratch_shapes=[pltpu.VMEM(shape, kind) for shape, kind in scratch],
            cost_estimate=pl.CostEstimate(flops=flops, bytes_accessed=0, transcendentals=0),
            compiler_params=pltpu.CompilerParams(vmem_limit_bytes=VMEM_BYTES),
        )(place, *args)

    near, keep, send = call(
        own_kernel,
        OWN_FLOPS,
        [((span, part), bf16), ((rows, span), jnp.float32), ((rows, span), bf16)],
        [((2 * rows, span), jnp.float32)],
        home, p1, p2a, p2b, p3a, p3b, far, fp, drow, dcol, dpair,
    )
    mine = (keep + tm_swap(send, 2).astype(jnp.float32)).astype(bf16)
    e1a, e1b = tm_swap(ea, 1), tm_swap(eb, 1)
    (cross,) = call(early_kernel, EARLY_FLOPS, [((rows, span), bf16)], [], near, ea, eb, drow, dcol)
    before = tm_swap(cross, 2)
    (pair,) = call(pair_kernel, PAIR_FLOPS, [((2 * rows, part), bf16)], [], ea, eb, e1a, e1b)
    (last,) = call(
        late_kernel,
        LATE_FLOPS,
        [((rows, span + 2 * rows), bf16)],
        [],
        near, late, pair, before, drow, dcol, dpair,
    )
    last, offsets, taper_index = lax.optimization_barrier((last, offsets, taper_index))
    w = weights(offsets, taper_index, me * freqs, freqs, order)
    pieces = everyone(pix_sum(jnp.concatenate([mine, last], axis=1)))
    gram_width = 2 * NB
    total_pixels = width * lax.axis_size("pix")
    gram, energy = call(
        functools.partial(finish_kernel, 1.0 / total_pixels),
        FINISH_FLOPS,
        [((freqs, gram_width, gram_width), jnp.float32), ((1, freqs), jnp.float32)],
        [((2 * span, 2 * span), bf16), ((freqs * gram_width, 2 * span), bf16)],
        w, *pieces,
    )
    return gram, energy.reshape(freqs)


def solution(mesh):
    placed = (P("tm", ("group", "pix", "sub")), P(), P())
    pairs = mesh.shape["tm"] == 8 and mesh.shape["pix"] == 2 and mesh.shape["sub"] == 1

    def shards(anomaly, offsets, taper_index):
        if pairs and anomaly.shape[0] == 64 and anomaly.shape[1] % 512 == 0:
            return covariance_shards(anomaly, offsets, taper_index)
        return spectra_shards(anomaly, offsets, taper_index)

    return jax.shard_map(
        shards,
        mesh=mesh,
        in_specs=placed,
        out_specs=(P(("group", "tm"), None, None), P(("group", "tm"))),
        check_vma=False,
    )
```

```python
import functools
import math

import jax
import jax.numpy as jnp
import numpy as np
from jax import lax
from jax.experimental import pallas as pl
from jax.experimental.pallas import tpu as pltpu
from jax.sharding import PartitionSpec as P

NFFT = 256
NB = 32
POWER = 8
NF = 128
VMEM_BYTES = 40 * 1024 * 1024
OWN_FLOPS, EARLY_FLOPS, PAIR_FLOPS, LATE_FLOPS, FINISH_FLOPS = 0, 0, 0, 4_000_000_000, 1_000_000_000
EARLY_LEAD = 4
SEATS = (0, 1, 4, 5, 6, 7, 2, 3)

power_eps = 1e-06


def window_rows(taper_index, length):
    steps_t = jnp.arange(length, dtype=jnp.float32)
    phase = steps_t * (2.0 * math.pi / length)
    center = (steps_t + 0.5) * (math.pi / length)
    hann = jnp.sin(center) ** 2
    hamming = 0.54 - 0.46 * jnp.cos(phase)
    blackman = 0.42 - 0.5 * jnp.cos(phase) + 0.08 * jnp.cos(2.0 * phase)
    sine_win = jnp.sin(center)
    table_rows = jnp.stack([hann, hamming, blackman, sine_win])
    chosen = jnp.zeros((taper_index.shape[0], length), jnp.float32)
    for which in range(4):
        chosen = chosen + jnp.where(
            taper_index[:, None] == which, table_rows[which][None, :], jnp.float32(0.0)
        )
    return chosen


def dft_table(length, kept):
    freqs = jnp.arange(kept, dtype=jnp.int32)
    times = jnp.arange(length, dtype=jnp.int32)
    product = freqs[:, None] * times[None, :] % length
    angle = product.astype(jnp.float32) * (2.0 * math.pi / length)
    return jnp.stack([jnp.cos(angle), -jnp.sin(angle)]).astype(jnp.bfloat16)


def local_gram(spectra):
    stacked = spectra.reshape(2 * spectra.shape[1], spectra.shape[2], spectra.shape[3])
    return jnp.einsum("ifp,jfp->fij", stacked, stacked, preferred_element_type=jnp.float32)


def spectra_shards(anomaly, offsets, taper_index):
    series = lax.all_to_all(anomaly, "tm", split_axis=1, concat_axis=0, tiled=True)
    windows = window_rows(taper_index, NFFT)
    energy = 1.0 / jnp.sqrt(jnp.sum(windows * windows, axis=1))
    transform = dft_table(NFFT, NF)
    width_here = series.shape[1]
    per_group = 8
    gram_width = 2 * NB

    def fill_group(position, buffer):
        first_block = position * per_group
        starts = lax.dynamic_slice_in_dim(offsets, first_block, per_group, 0)
        shapes = lax.dynamic_slice_in_dim(windows, first_block, per_group, 0)
        scales = lax.dynamic_slice_in_dim(energy, first_block, per_group, 0)
        segments = jax.vmap(lambda first_day: lax.dynamic_slice_in_dim(series, first_day, NFFT, 0))(
            starts
        )
        windowed = (segments * shapes[:, :, None]).astype(jnp.bfloat16)
        spectra = jnp.einsum(
            "rkt,btp->rbkp", transform, windowed, preferred_element_type=jnp.float32
        )
        spectra = (spectra * scales[None, :, None, None]).astype(jnp.bfloat16)
        return lax.dynamic_update_slice_in_dim(buffer, spectra, first_block, 1)

    empty = jnp.zeros((2, NB, NF, width_here), jnp.bfloat16)
    spectra = lax.fori_loop(0, NB // per_group, fill_group, empty)
    received = lax.all_to_all(spectra, "tm", split_axis=2, concat_axis=3, tiled=True)
    partial_value = local_gram(received)
    summed = lax.psum(partial_value, ("pix", "sub"))
    total_pixels = anomaly.shape[1] * lax.axis_size(("pix", "sub"))
    spectral_gram = summed / total_pixels
    vector = jnp.ones((spectral_gram.shape[0], gram_width), jnp.float32)
    for _ in range(POWER):
        applied = jnp.einsum("fij,fj->fi", spectral_gram, vector, precision=lax.Precision.HIGHEST)
        vector = applied / jnp.sqrt(jnp.mean(applied * applied, axis=1, keepdims=True) + power_eps)
    applied = jnp.einsum("fij,fj->fi", spectral_gram, vector, precision=lax.Precision.HIGHEST)
    leading_energy = jnp.sqrt(jnp.mean(applied * applied, axis=1))
    return (spectral_gram, leading_energy)


def day_factors(days):
    return (1.0 + 0.4 * ((np.arange(days) * 0.6180339887498949) % 1.0)).astype(np.float32)


def day_order(rows):
    blocks = [4 * half + 2 * chip + core for half in (0, 1) for core in (0, 1) for chip in (0, 1)]
    return np.concatenate([np.arange(rows) + rows * block for block in blocks]).astype(np.int32)


def weights(offsets, taper_index, first_freq, freqs, order):
    days = order.shape[0]
    day = jnp.asarray(order)
    local = day[None, :] - offsets[:, None]
    inside = (local >= 0) & (local < NFFT)
    steps_t = local.astype(jnp.float32)
    phase = steps_t * (2.0 * math.pi / NFFT)
    center = (steps_t + 0.5) * (math.pi / NFFT)
    sine_win = jnp.sin(center)
    table = [
        sine_win**2,
        0.54 - 0.46 * jnp.cos(phase),
        0.42 - 0.5 * jnp.cos(phase) + 0.08 * jnp.cos(2.0 * phase),
        sine_win,
    ]
    window = jnp.zeros(local.shape, jnp.float32)
    for which in range(4):
        window = window + jnp.where(taper_index[:, None] == which, table[which], 0.0)
    window = jnp.where(inside, window, 0.0)
    energy = 1.0 / jnp.sqrt(jnp.sum(window * window, axis=1, keepdims=True))
    factors = day_factors(days // 2)
    window = window * energy * (1.0 / np.concatenate([factors, factors]))[None, :]

    def turn(steps):
        freq = first_freq + jnp.arange(freqs, dtype=jnp.int32)
        angle = ((freq[:, None] * steps[None, :]) % NFFT).astype(jnp.float32)
        angle = angle * (2.0 * math.pi / NFFT)
        return jnp.cos(angle), jnp.sin(angle)

    cos_t, sin_t = lax.optimization_barrier(turn(day))
    cos_b, sin_b = lax.optimization_barrier(turn(offsets))
    window = lax.optimization_barrier(window)
    ct, st = cos_t[:, None, :], sin_t[:, None, :]
    cb, sb = cos_b[:, :, None], sin_b[:, :, None]
    real = window * (ct * cb + st * sb)
    imag = window * (ct * sb - st * cb)
    return jnp.concatenate([real, imag], axis=1).astype(jnp.bfloat16)


def outer(left, right):
    return lax.dot_general(left, right, (((1,), (1,)), ((), ())), preferred_element_type=jnp.float32)


def spread(pair, chip):
    low = lax.broadcasted_iota(jnp.int32, pair.shape, 1) < pair.shape[1] // 2
    turned = pltpu.roll(pair, pair.shape[1] // 2, 1)
    first = jnp.where(chip == 0, pair, turned)
    second = jnp.where(chip == 0, turned, pair)
    keep = low == (chip == 0)
    return jnp.concatenate([jnp.where(keep, first, 0.0), jnp.where(keep, second, 0.0)], axis=1)


def block(index, rows):
    return pl.ds(pl.multiple_of(index * rows, rows), rows)


def own_kernel(place, p0, p1, p2a, p2b, p3a, p3b, far, fp, drow, dcol, dpair, near, keep, send, strip):
    chip, core = place[1], place[2]
    slot = 2 * core + chip
    rows, middle = p2a.shape
    near[block(slot, rows), :] = p0[...]
    near[block(slot ^ 2, rows), :] = p1[...]
    for flip, first, second in ((1, p2a, p2b), (3, p3a, p3b)):
        near[block(slot ^ flip, rows), :middle] = first[...]
        near[block(slot ^ flip, rows), middle:] = second[...]
    mine = block(core, 2 * rows)
    strip[...] = outer(near[mine, :], near[...]) * (0.5 * dcol[mine, :]) * drow[...]
    same = 0.5 * outer(far[...], far[...])
    cross = outer(far[:, block(core, fp.shape[1])], fp[...])
    inside = jnp.where(core == 0, jnp.concatenate([same, cross], axis=1), jnp.concatenate([cross, same], axis=1))
    inside = inside * dcol[block(slot, rows), :] * dpair[chip]
    keep[...] = strip[block(chip, rows), :] + spread(inside, chip)
    send[...] = strip[block(1 - chip, rows), :].astype(jnp.bfloat16)


def early_kernel(place, near, ea, eb, drow, dcol, out):
    rows, cut = ea.shape
    slot = 2 * place[2] + 1 - place[1]
    value = outer(ea[...], near[:, :cut]) + outer(eb[...], near[:, cut:])
    out[...] = (value * dcol[block(slot, rows), :] * drow[...]).astype(jnp.bfloat16)


def pair_kernel(place, e0a, e0b, e1a, e1b, pair):
    (rows, cut), core = e0a.shape, place[2]
    for index, first, second in ((core, e0a, e0b), (1 - core, e1a, e1b)):
        pair[block(index, rows), :cut] = first[...]
        pair[block(index, rows), cut:] = second[...]


def late_kernel(place, near, late, pair, before, drow, dcol, dpair, out):
    rows, span = late.shape[0], near.shape[0]
    chip, core = place[1], place[2]
    scale = dcol[block(2 * core + chip, rows), :]
    cross = outer(late[...], near[...]) * scale * drow[...] + before[...].astype(jnp.float32)
    out[:, :span] = cross.astype(jnp.bfloat16)
    out[:, span:] = (outer(late[...], pair[...]) * scale * dpair[1 - chip]).astype(jnp.bfloat16)


def finish_kernel(scale, place, w, *refs):
    pieces, (gram, energy, table, y, packed) = refs[:8], refs[8:]
    rows, span = pieces[0].shape[0], table.shape[0] // 2
    for d in range(8):
        half, chip, core = place[0] ^ (d >> 2), place[1] ^ ((d >> 1) & 1), place[2] ^ (d & 1)
        mine, other = pieces[SEATS.index(d)], pieces[SEATS.index(d ^ 4)]
        at = block(4 * half + 2 * core + chip, rows)
        extra = spread(other[:, 2 * span :].astype(jnp.float32), 1 - chip)
        table[at, block(half, span)] = (mine[:, :span].astype(jnp.float32) + extra).astype(jnp.bfloat16)
        table[at, block(1 - half, span)] = other[:, span : 2 * span]
    freqs, width, days = w.shape
    flat = w[...].reshape(freqs * width, days)
    y[...] = jnp.dot(flat, table[...], preferred_element_type=jnp.float32).astype(jnp.bfloat16)
    pair = 2 * width
    low = lax.broadcasted_iota(jnp.int32, (1, 1, pair), 2) < width
    for k in range(freqs // 2):
        rows_k = slice(k * pair, (k + 1) * pair)
        part = outer(y[rows_k, :], flat[rows_k, :]) * scale
        part = part + part.T
        top, bottom = part[:width, :], part[width:, :]
        packed[k] = jnp.where(low[0], top, bottom)
        gram[2 * k] = top[:, :width]
        gram[2 * k + 1] = pltpu.roll(bottom, width, 1)[:, :width]

    def halves(value):
        left = jnp.sum(jnp.where(low, value, 0.0), axis=2, keepdims=True)
        return left, jnp.sum(jnp.where(low, 0.0, value), axis=2, keepdims=True)

    g = packed[...]
    vector = jnp.ones((freqs // 2, 1, pair), jnp.float32)
    for step in range(POWER + 1):
        if step % 2 == 0:
            applied = jnp.sum(g * vector, axis=1, keepdims=True)
            first, second = (m * (1.0 / width) for m in halves(applied * applied))
            vector = applied * lax.rsqrt(jnp.where(low, first, second) + power_eps)
        else:
            left, right = halves(g * vector)
            first = jnp.sum(left * left, axis=1, keepdims=True) * (1.0 / width)
            second = jnp.sum(right * right, axis=1, keepdims=True) * (1.0 / width)
            vector = jnp.where(low, left * lax.rsqrt(first + power_eps), right * lax.rsqrt(second + power_eps))
    lane = lax.broadcasted_iota(jnp.int32, (freqs // 2, 1, freqs), 2)
    even = 2 * lax.broadcasted_iota(jnp.int32, (freqs // 2, 1, freqs), 0)
    both = jnp.where(lane == even, jnp.sqrt(first), 0.0) + jnp.where(lane == even + 1, jnp.sqrt(second), 0.0)
    energy[...] = jnp.sum(both, axis=0)


def covariance_shards(anomaly, offsets, taper_index):
    n = lax.axis_size("tm")
    me = lax.axis_index("tm")
    half, chip, core = me // 4, (me // 2) % 2, me % 2
    place = jnp.stack([half, chip, core]).astype(jnp.int32)
    rows, width = anomaly.shape
    span, part = 4 * rows, width // 4
    order = day_order(rows)
    freqs = NF // n
    bf16 = jnp.bfloat16

    def tm_swap(value, bit):
        return lax.ppermute(value, "tm", [(i, i ^ bit) for i in range(n)])

    def pix_sum(value):
        other = lax.ppermute(value, "pix", [(0, 1), (1, 0)])
        return (value.astype(jnp.float32) + other.astype(jnp.float32)).astype(bf16)

    def everyone(value):
        return [v for bits in SEATS[::2] for v in with_core(value if bits == 0 else tm_swap(value, bits))]

    def with_core(value):
        return value, tm_swap(value, 1)

    def cut(source, start, count):
        return lax.optimization_barrier((source, lax.dynamic_slice_in_dim(source, start, count, 1)))

    z = me // 2
    lead = part * EARLY_LEAD // 16
    source, home = cut(anomaly, z * part, part)
    source, far6a = cut(source, (z ^ 3) * part, lead)
    ea = tm_swap(far6a, 6)
    p1 = tm_swap(home, 1)
    source, p1 = lax.optimization_barrier((source, p1))
    source, far6b = cut(source, (z ^ 3) * part + lead, part - lead)
    eb = tm_swap(far6b, 6)
    source, side_a = cut(source, (z ^ 1) * part, part // 2)
    source, side_b = cut(source, (z ^ 1) * part + part // 2, part // 2)
    source, away = cut(source, (2 * (1 - half) + 1 - core) * part, part)
    source, far = cut(source, (1 - half) * 2 * part, 2 * part)
    p2a, p2b = tm_swap(side_a, 2), tm_swap(side_b, 2)
    fp = tm_swap(away, 1)
    source, far4 = cut(source, (z ^ 2) * part, part)
    far4, ea = lax.optimization_barrier((far4, ea))
    late = tm_swap(far4, 4)
    p3a, p3b = tm_swap(p2a, 1), tm_swap(p2b, 1)

    factors = day_factors(span)
    first, second = factors[: 2 * rows].reshape(2, rows), factors[2 * rows :].reshape(2, rows)
    pairs = np.concatenate([first, second], axis=1)[:, None, :]
    drow, dcol, dpair = jnp.asarray(factors[None, :]), jnp.asarray(factors[:, None]), jnp.asarray(pairs)
    vmem = pl.BlockSpec(memory_space=pltpu.VMEM)
    smem = pl.BlockSpec(memory_space=pltpu.SMEM)

    def call(kernel, flops, outs, scratch, *args):
        return pl.pallas_call(
            kernel,
            out_shape=[jax.ShapeDtypeStruct(shape, kind) for shape, kind in outs],
            in_specs=[smem] + [vmem] * len(args),
            out_specs=[vmem] * len(outs),
            scratch_shapes=[pltpu.VMEM(shape, kind) for shape, kind in scratch],
            cost_estimate=pl.CostEstimate(flops=flops, bytes_accessed=0, transcendentals=0),
            compiler_params=pltpu.CompilerParams(vmem_limit_bytes=VMEM_BYTES),
        )(place, *args)

    near, keep, send = call(
        own_kernel,
        OWN_FLOPS,
        [((span, part), bf16), ((rows, span), jnp.float32), ((rows, span), bf16)],
        [((2 * rows, span), jnp.float32)],
        home, p1, p2a, p2b, p3a, p3b, far, fp, drow, dcol, dpair,
    )
    mine = (keep + tm_swap(send, 2).astype(jnp.float32)).astype(bf16)
    e1a, e1b = tm_swap(ea, 1), tm_swap(eb, 1)
    (cross,) = call(early_kernel, EARLY_FLOPS, [((rows, span), bf16)], [], near, ea, eb, drow, dcol)
    before = tm_swap(cross, 2)
    (pair,) = call(pair_kernel, PAIR_FLOPS, [((2 * rows, part), bf16)], [], ea, eb, e1a, e1b)
    (last,) = call(
        late_kernel,
        LATE_FLOPS,
        [((rows, span + 2 * rows), bf16)],
        [],
        near, late, pair, before, drow, dcol, dpair,
    )
    last, offsets, taper_index = lax.optimization_barrier((last, offsets, taper_index))
    w = weights(offsets, taper_index, me * freqs, freqs, order)
    pieces = everyone(pix_sum(jnp.concatenate([mine, last], axis=1)))
    gram_width = 2 * NB
    total_pixels = width * lax.axis_size("pix")
    gram, energy = call(
        functools.partial(finish_kernel, 1.0 / total_pixels),
        FINISH_FLOPS,
        [((freqs, gram_width, gram_width), jnp.float32), ((1, freqs), jnp.float32)],
        [
            ((2 * span, 2 * span), bf16),
            ((freqs * gram_width, 2 * span), bf16),
            ((freqs // 2, gram_width, 2 * gram_width), jnp.float32),
        ],
        w, *pieces,
    )
    return gram, energy.reshape(freqs)


def solution(mesh):
    placed = (P("tm", ("group", "pix", "sub")), P(), P())
    pairs = mesh.shape["tm"] == 8 and mesh.shape["pix"] == 2 and mesh.shape["sub"] == 1

    def shards(anomaly, offsets, taper_index):
        if pairs and anomaly.shape[0] == 64 and anomaly.shape[1] % 512 == 0:
            return covariance_shards(anomaly, offsets, taper_index)
        return spectra_shards(anomaly, offsets, taper_index)

    return jax.shard_map(
        shards,
        mesh=mesh,
        in_specs=placed,
        out_specs=(P(("group", "tm"), None, None), P(("group", "tm"))),
        check_vma=False,
    )
```
